256 devices in a mesh: ctx: 32 (over z, y_lo, core), head: 8 (over x, y_hi).
Axes of the slice: x: 4, y: 4 (y_hi: 2, y_lo: 2; y = y_hi * 2 + y_lo), z: 8, core: 2. Of those that a mesh axis runs over, the one named last changes fastest.
Arguments:
- query_nope: bfloat16 [8192, 16384], P('ctx', 'head'), may hold values from -6 to 6
- query_rope: bfloat16 [8192, 8192], P('ctx', 'head'), may hold values from -300 to 300, as said below
- latent: bfloat16 [8192, 576], P(('ctx', 'head')), may hold values from -6 to 6, as said below
- key_up: bfloat16 [512, 16384], P(None, 'head'), may hold values from -0.25 to 0.25
- value_up: bfloat16 [512, 16384], P(None, 'head'), may hold values from -0.25 to 0.25
- doc_lengths: int32 [8], replicated, may hold values from 1 to 3072, 8192 in all
- owner: int32 [8192], P('ctx'), may hold values from 0 to 8191, as said below
Outputs:
- attended: bfloat16 [8192, 16384], P('ctx', 'head')
The draws below stay inside these ranges and needn't reach their ends.
Inputs may be any that keep to these rules, and one draw needn't show every extreme that they name: `doc_lengths`: positive lengths that sum to 8192; the longest is exactly 3072. `owner`: a permutation of the rows; the 256 tokens of each block of the sequence go in equal numbers to every block's rows. `latent`: finite values. `query_rope`: finite values.
All inputs are finite; a program needn't handle non-finite values.
Results may differ from the reference program's by a relative error of at most 0.0058.
Values may be sent and summed in bfloat16 or wider, within the bound.
A program may use at most 128 MiB of HBM per device.

```python
import math
import jax
import jax.numpy as jnp
import numpy as np
from jax import lax

LATENT = 512
ROPE = 64
NOPE = 128
VDIM = 128
TOK_DEV = 256
DOCS = 8
HEADS = 128
TOKENS = 8192
WINDOW = 1024
MOST_DOC = 3072
N_CTX = 32


def shared_latent(key, spread):
    key_normal = jax.random.fold_in(key, 0)
    key_scale = jax.random.fold_in(key, 2)
    normal = jnp.clip(jax.random.normal(key_normal, (TOKENS, LATENT + ROPE), jnp.float32), -6.0, 6.0)
    values = normal
    scales = jnp.exp(jax.random.uniform(key_scale, (TOKENS, 1), jnp.float32, -math.log(spread), 1e-09))
    values = values * scales
    rope = values[:, LATENT:]
    return jnp.concatenate([values[:, :LATENT], rope], axis=1)


def draw_latent(key, part):
    values = shared_latent(key, 1.0)
    return values.astype(jnp.bfloat16)


def draw_query_rope(key, part):
    own_key = jax.random.fold_in(key, 7)
    return jnp.clip(jax.random.normal(own_key, (TOKENS, HEADS * ROPE), jnp.float32), -6.0, 6.0).astype(jnp.bfloat16)


def draw_owner(key, part):
    key = jax.random.fold_in(key, 5)
    blocks = TOKENS // TOK_DEV
    key_send, key_take = jax.random.split(key)
    send = jax.vmap(lambda k: jax.random.permutation(k, TOK_DEV))(jax.random.split(key_send, blocks))
    take = jax.vmap(lambda k: jax.random.permutation(k, TOK_DEV))(jax.random.split(key_take, blocks))
    source = jnp.arange(blocks)[:, None]
    dest = (send + source) % blocks
    slot = source * (TOK_DEV // blocks) + send // blocks
    final = take[dest, slot]
    return (dest * TOK_DEV + final).reshape(TOKENS).astype(jnp.int32)


def levels(rng, shape, shards, least, high):
    def one(position, shards_of):
        draws = jax.random.uniform(jax.random.fold_in(jax.random.fold_in(rng, 6), position), (shards_of,), jnp.float32, least / len(shards), high / len(shards))
        return jnp.repeat(jnp.exp(draws), shape[position] // shards_of).reshape((-1,) + (1,) * (len(shape) - position - 1))

    level = one(*shards[0])
    for cut in shards[1:]:
        level = level * one(*cut)
    return level


def split_up(number_of, total, reach, skew):
    loads = [(1 << 20) // math.isqrt(rank ** skew) + 1 for rank in range(2, number_of + 1)]
    surplus, holding = total - reach - (number_of - 1), [1] * (number_of - 1)
    while surplus > 0:
        candidates = [i for i in range(number_of - 1) if holding[i] < reach]
        whole, budget = sum([loads[i] for i in candidates]), surplus
        for i in candidates:
            extra = min(reach - holding[i], max(1, budget * loads[i] // whole), surplus)
            holding[i] = holding[i] + extra
            surplus = surplus - extra
    return np.array([reach] + holding)


def ragged_sizes(key, count, total, reach, skew):
    if count == 2:
        one = jax.random.randint(key, (), max(1, total - reach), min(reach, total - 1) + 1)
        return jnp.stack([one, total - one])
    sizes = jnp.asarray(split_up(count, total, reach, skew), jnp.int32)
    couples = (count - 1) // 2
    source_of, sink = sizes[1:1 + 2 * couples:2], sizes[2:2 + 2 * couples:2]
    room = jnp.minimum(source_of - 1, reach - sink)
    passed = jax.random.randint(jax.random.fold_in(key, 1), (couples,), 0, 1 << 20) % (room + 1)
    sizes = sizes.at[1:1 + 2 * couples:2].set(source_of - passed).at[2:2 + 2 * couples:2].set(sink + passed)
    return sizes[jax.random.permutation(jax.random.fold_in(key, 2), count)]


def normal_values(key, shape, width, reach, shards=(), held_as=jnp.bfloat16):
    gain = levels(key, shape, shards, -0.22, 0.18) if shards else 1.0
    drawn = jax.random.normal(key, shape, jnp.float32) * width * gain
    return jnp.minimum(jnp.maximum(drawn, -reach), reach).astype(held_as)


def setup_inputs(seed: int = 0) -> dict:
    key_of = jax.random.split(jax.random.key(seed), 8)
    query_nope = normal_values(key_of[0], (TOKENS, HEADS * NOPE), 1.0, 6.0, ((0, 32), (1, 8)))
    query_rope = draw_query_rope(jax.random.fold_in(key_of[7], 71), 0)
    latent = draw_latent(jax.random.fold_in(key_of[7], 71), 0)
    key_up = normal_values(key_of[3], (LATENT, HEADS * NOPE), LATENT ** -0.5, 0.25, ((1, 8),))
    value_up = normal_values(key_of[4], (LATENT, HEADS * VDIM), LATENT ** -0.5, 0.25, ((1, 8),))
    doc_lengths = ragged_sizes(key_of[5], DOCS, TOKENS, MOST_DOC, 2).astype(jnp.int32)
    owner = draw_owner(jax.random.fold_in(key_of[7], 71), 0)
    return dict(query_nope=query_nope, query_rope=query_rope, latent=latent, key_up=key_up, value_up=value_up, doc_lengths=doc_lengths, owner=owner)


def segment_of(positions, doc_lengths):
    ends = jnp.cumsum(doc_lengths).astype(jnp.int32)
    return jnp.sum((ends[None, :] <= positions[:, None]).astype(jnp.int32), axis=1)


def reference(query_nope, query_rope, latent, key_up, value_up, doc_lengths, owner):
    scale = 1.0 / (float(NOPE + ROPE) ** 0.5)
    compressed = latent[:, :LATENT]
    keys_nope = jnp.dot(compressed, key_up, preferred_element_type=jnp.float32).astype(jnp.bfloat16)
    values = jnp.dot(compressed, value_up, preferred_element_type=jnp.float32).astype(jnp.bfloat16)
    keys_pad = jnp.concatenate([jnp.zeros((WINDOW, HEADS * NOPE), jnp.bfloat16), keys_nope], axis=0)
    values_pad = jnp.concatenate([jnp.zeros((WINDOW, HEADS * VDIM), jnp.bfloat16), values], axis=0)
    rope_pad = jnp.concatenate([jnp.zeros((WINDOW, ROPE), jnp.bfloat16), latent[:, LATENT:]], axis=0)
    span = WINDOW + TOK_DEV

    def one_block(block):
        start = (block * TOK_DEV).astype(jnp.int32)
        query_rows = lax.dynamic_slice_in_dim(query_nope, start, TOK_DEV, 0)
        rope_rows = lax.dynamic_slice_in_dim(query_rope, start, TOK_DEV, 0)
        key_rows = lax.dynamic_slice_in_dim(keys_pad, start, span, 0)
        value_rows = lax.dynamic_slice_in_dim(values_pad, start, span, 0)
        key_rope = lax.dynamic_slice_in_dim(rope_pad, start, span, 0)
        query_pos = start + jnp.arange(TOK_DEV, dtype=jnp.int32)
        key_pos = start - WINDOW + jnp.arange(span, dtype=jnp.int32)
        query_seg = segment_of(query_pos, doc_lengths)
        key_seg = segment_of(jnp.maximum(key_pos, 0), doc_lengths)
        offset = query_pos[:, None] - key_pos[None, :]
        visible = (key_pos[None, :] >= 0) & (offset >= 0) & (offset < WINDOW) & (query_seg[:, None] == key_seg[None, :])

        def one_head(head):
            head = head.astype(jnp.int32)
            q_part = lax.dynamic_slice_in_dim(query_rows, head * NOPE, NOPE, 1)
            r_part = lax.dynamic_slice_in_dim(rope_rows, head * ROPE, ROPE, 1)
            k_part = lax.dynamic_slice_in_dim(key_rows, head * NOPE, NOPE, 1)
            v_part = lax.dynamic_slice_in_dim(value_rows, head * VDIM, VDIM, 1)
            scores = jnp.dot(q_part, k_part.T, preferred_element_type=jnp.float32)
            scores = scores + jnp.dot(r_part, key_rope.T, preferred_element_type=jnp.float32)
            masked = jnp.where(visible, scores * scale, -1e30)
            largest = jnp.max(masked, axis=1, keepdims=True)
            probs = jnp.where(visible, jnp.exp(masked - largest), 0.0)
            total = jnp.sum(probs, axis=1, keepdims=True)
            summed = jnp.dot(probs.astype(jnp.bfloat16), v_part, preferred_element_type=jnp.float32)
            return (summed / total).astype(jnp.bfloat16)

        per_head = lax.map(one_head, jnp.arange(HEADS, dtype=jnp.int32))
        return jnp.transpose(per_head, (1, 0, 2)).reshape(TOK_DEV, HEADS * VDIM)

    blocks = lax.map(one_block, jnp.arange(N_CTX, dtype=jnp.int32))
    result = blocks.reshape(TOKENS, HEADS * VDIM)
    return jnp.zeros((TOKENS, HEADS * VDIM), jnp.bfloat16).at[owner].set(result)
```

```python
import functools

import jax
import jax.numpy as jnp
from jax import lax
from jax.experimental import pallas as pl
from jax.experimental.pallas import tpu as pltpu
from jax.sharding import PartitionSpec as P

LATENT = 512
ROPE = 64
NOPE = 128
ROWS = 256
N_CTX = 32
N_HEAD = 8
SHARD = 32
BLOCKS = 5
SPAN = BLOCKS * ROWS
WINDOW = 1024
GROUPS = 8
SLOT = 8
DOCS = 8
FAR = -1e30
TO_EXP2 = 1.4426950408889634 / float(NOPE + ROPE) ** 0.5
MESH = pl.DeviceIdType.MESH
F32 = jnp.float32
BF16 = jnp.bfloat16


def iota(shape, dim):
    return lax.broadcasted_iota(jnp.int32, shape, dim)


def kernel(
    qn_hbm, qr_hbm, lat_hbm, ku_hbm, vu_hbm, docs, owner_ref, out_ref,
    qn, qr, ku, vu, stage, buf, kr, qbits, perm, place, outb, inb, idx_out, idx_in,
    load_sem, own_sem, gsend, grecv, fsend, isend, irecv, asend, arecv,
):
    c = lax.axis_index("ctx")
    h = lax.axis_index("head")
    k = lax.rem(c, 2)
    sibling = (c + 1 - 2 * k, h)

    def at(ahead, heads_on):
        return (lax.rem(c + ahead + N_CTX, N_CTX), lax.rem(h + heads_on, N_HEAD))

    lat_in = pltpu.make_async_copy(lat_hbm, stage, load_sem.at[0])
    lat_in.start()
    loads = [
        pltpu.make_async_copy(src, dst, load_sem.at[1 + i])
        for i, (src, dst) in enumerate(((ku_hbm, ku), (vu_hbm, vu), (qn_hbm, qn), (qr_hbm, qr)))
    ]
    for load in loads:
        load.start()

    barrier = pltpu.get_barrier_semaphore()

    def greet_ctx(i, carry):
        pl.semaphore_signal(barrier, inc=1, device_id=at(i, 0), device_id_type=MESH)
        return carry

    lax.fori_loop(1, N_CTX, greet_ctx, 0)

    def greet_head(j, carry):
        for ahead in (0, 2, -2, 4, -4):
            pl.semaphore_signal(barrier, inc=1, device_id=at(ahead, j), device_id_type=MESH)
        return carry

    lax.fori_loop(1, N_HEAD, greet_head, 0)
    pl.semaphore_wait(barrier, N_CTX - 1 + 5 * (N_HEAD - 1))

    lat_in.wait()
    own = pltpu.make_async_copy(stage, buf.at[4, h], grecv.at[4])
    own.start()
    for n, (ahead, slot, first) in enumerate(((2, 2, 0), (0, 4, 1), (4, 0, 0))):

        def spread(j, carry, n=n, ahead=ahead, slot=slot):
            pltpu.make_async_remote_copy(
                stage, buf.at[slot, h], gsend.at[n], grecv.at[slot],
                device_id=at(ahead, j), device_id_type=MESH,
            ).start()
            return carry

        lax.fori_loop(first, N_HEAD, spread, 0)

    owner = owner_ref[...]
    row = lax.shift_right_logical(owner, 8)
    place_row = jnp.bitwise_and(owner, ROWS - 1)
    step_row = jnp.bitwise_and(row - c + (2 * N_CTX - 1), N_CTX - 1)
    step_all = jnp.broadcast_to(step_row, (ROWS, ROWS))
    sub = iota((ROWS, ROWS), 0)
    lane = iota((ROWS, ROWS), 1)
    step_col = jnp.sum(jnp.where(sub == lane, step_all, 0), axis=1, keepdims=True)
    same = (step_col == step_row) & (sub < lane)
    rank = jnp.sum(jnp.where(same, 1, 0), axis=0, keepdims=True)
    slot_row = step_row * SLOT + rank
    hit = sub == slot_row
    perm[...] = jnp.where(hit, 1.0, 0.0).astype(BF16)
    place_col = jnp.sum(jnp.where(hit, place_row, 0), axis=1, keepdims=True)
    idx = jnp.broadcast_to(place_col, (ROWS, 128)).reshape(N_CTX, SLOT, 128)
    idx_out[...] = idx
    idx_in[N_CTX - 1] = idx[N_CTX - 1]

    def send_idx(i, carry):
        pltpu.make_async_remote_copy(
            idx_out.at[i], idx_in.at[i], isend, irecv,
            device_id=at(i + 1, 0), device_id_type=MESH,
        ).start()
        return carry

    lax.fori_loop(0, N_CTX - 1, send_idx, 0)

    lanes = iota((1, ROPE), 1)
    starts = jnp.zeros((1, ROPE), jnp.int32)
    ends = jnp.zeros((1, ROPE), jnp.int32)
    total = 0
    for d in range(DOCS):
        starts = jnp.where(lanes == d, total, starts)
        total = total + docs[d]
        ends = jnp.where(lanes == d, total, ends)
    key_pos = (c - 4) * ROWS + iota((SPAN, ROPE), 0)
    key_in = (key_pos >= starts) & (key_pos < ends)
    key_bits = jnp.where(key_in | (iota((SPAN, ROPE), 1) >= DOCS), 0.0, 1.0).astype(BF16)
    query_pos = c * ROWS + iota((ROWS, ROPE), 0)
    query_in = (query_pos >= starts) & (query_pos < ends)
    query_bits = jnp.where(query_in, FAR, 0.0)
    zeros = jnp.zeros((ROWS, ROPE), F32)
    ones = jnp.ones((ROWS, ROPE), F32)
    qbits[0] = jnp.concatenate([zeros, query_bits], axis=1).astype(BF16)
    qbits[1] = jnp.concatenate([query_bits, zeros], axis=1).astype(BF16)
    qbits[2] = jnp.concatenate([ones, zeros], axis=1).astype(BF16)
    qbits[3] = jnp.concatenate([zeros, ones], axis=1).astype(BF16)

    def arrived(slot):
        pltpu.make_async_copy(buf.at[slot], buf.at[slot], grecv.at[slot]).wait()

    def forward(src, dst, n):
        return pltpu.make_async_remote_copy(
            buf.at[src], buf.at[dst], fsend.at[n], grecv.at[dst],
            device_id=sibling, device_id_type=MESH,
        )

    arrived(2)
    first = forward(2, 2 * k + 1, 0)
    first.start()
    other = 4 - 4 * k
    arrived(other)
    second = forward(other, 3 - 2 * k, 1)
    second.start()
    arrived(4 * k)
    arrived(1)
    arrived(3)
    for load in loads:
        load.wait()

    rope = buf[:, :, :, LATENT:].reshape(SPAN, ROPE)
    kr[0] = jnp.concatenate([rope, key_bits], axis=1)
    kr[1] = jnp.concatenate([key_bits, rope], axis=1)

    lower = lane <= sub

    def attend(g, carry):
        cols = pl.ds(pl.multiple_of(g * 2 * NOPE, 2 * NOPE), 2 * NOPE)
        latent = buf[:, :, :, :LATENT].reshape(SPAN, LATENT)
        keys = jnp.dot(latent, ku[:, cols], preferred_element_type=F32).astype(BF16)
        values = jnp.dot(latent, vu[:, cols], preferred_element_type=F32).astype(BF16)
        q_two = qn[:, cols]
        r_two = qr[:, pl.ds(pl.multiple_of(g * 2 * ROPE, 2 * ROPE), 2 * ROPE)]
        outs = []
        for e in range(2):
            part = slice(e * NOPE, (e + 1) * NOPE)
            kx = jnp.concatenate([keys[:, part], kr[e]], axis=1)
            qx = jnp.concatenate([q_two[:, part], r_two * qbits[2 + e] + qbits[e]], axis=1)
            s = lax.dot_general(qx, kx, (((1,), (1,)), ((), ())), preferred_element_type=F32)
            s = jnp.concatenate(
                [
                    jnp.where(lower, FAR, s[:, :ROWS]),
                    s[:, ROWS:WINDOW],
                    jnp.where(lower, s[:, WINDOW:], FAR),
                ],
                axis=1,
            )
            largest = jnp.max(s, axis=1, keepdims=True)
            p = jnp.exp2((s - largest) * TO_EXP2)
            weight = jnp.sum(p, axis=1, keepdims=True)
            o = jnp.dot(p.astype(BF16), values[:, part], preferred_element_type=F32)
            outs.append((o / weight).astype(BF16))
        both = jnp.concatenate(outs, axis=1)
        sorted_ = jnp.dot(perm[...], both, preferred_element_type=F32)
        sorted_ = sorted_.reshape(N_CTX, SLOT, 2 * NOPE)
        packed = jnp.concatenate([sorted_[:, :, :NOPE], sorted_[:, :, NOPE:]], axis=1).astype(BF16)
        outb[g] = packed
        inb[g, N_CTX - 1] = packed[N_CTX - 1]

        def send(i, carry):
            pltpu.make_async_remote_copy(
                outb.at[g, i], inb.at[g, i], asend.at[g], arecv.at[g],
                device_id=at(i + 1, 0), device_id_type=MESH,
            ).start()
            return carry

        lax.fori_loop(0, N_CTX - 1, send, 0)
        return carry

    lax.fori_loop(0, GROUPS, attend, 0)

    rest = pl.ds(0, N_CTX - 1)
    pltpu.make_async_copy(idx_in.at[rest], idx_in.at[rest], irecv).wait()
    goal = idx_in[...].reshape(ROWS, 128)
    goal = jnp.concatenate([goal, goal], axis=1)
    place[...] = jnp.where(goal == lane, 1.0, 0.0).T.astype(BF16)

    def settle(g, carry):
        cols = pl.ds(pl.multiple_of(g * 2 * NOPE, 2 * NOPE), 2 * NOPE)
        pltpu.make_async_copy(inb.at[g, rest], inb.at[g, rest], arecv.at[g]).wait()
        got = inb[g].astype(F32)
        got = jnp.concatenate([got[:, :SLOT], got[:, SLOT:]], axis=2).reshape(ROWS, 2 * NOPE)
        out_ref[:, cols] = jnp.dot(
            place[...], got.astype(BF16), preferred_element_type=F32
        ).astype(BF16)
        return carry

    lax.fori_loop(0, GROUPS, settle, 0)

    def sent(ref, sem):
        pltpu.make_async_copy(ref, ref, sem).wait()

    sent(buf.at[0], gsend.at[0])
    sent(buf.at[0, pl.ds(0, N_HEAD - 1)], gsend.at[1])
    sent(buf.at[0], gsend.at[2])
    sent(buf.at[0], fsend.at[0])
    sent(buf.at[0], fsend.at[1])
    sent(idx_out.at[rest], isend)

    def all_sent(g, carry):
        sent(outb.at[g, rest], asend.at[g])
        return carry

    lax.fori_loop(0, GROUPS, all_sent, 0)


def per_device(query_nope, query_rope, latent, key_up, value_up, doc_lengths, owner):
    hbm = pl.BlockSpec(memory_space=pltpu.HBM)
    vmem = pl.BlockSpec(memory_space=pltpu.VMEM)
    dma = pltpu.SemaphoreType.DMA
    return pl.pallas_call(
        kernel,
        out_shape=jax.ShapeDtypeStruct(query_nope.shape, BF16),
        in_specs=[hbm] * 5 + [pl.BlockSpec(memory_space=pltpu.SMEM), vmem],
        out_specs=vmem,
        scratch_shapes=[
            pltpu.VMEM(query_nope.shape, BF16),
            pltpu.VMEM(query_rope.shape, BF16),
            pltpu.VMEM(key_up.shape, BF16),
            pltpu.VMEM(value_up.shape, BF16),
            pltpu.VMEM((SHARD, LATENT + ROPE), BF16),
            pltpu.VMEM((BLOCKS, N_HEAD, SHARD, LATENT + ROPE), BF16),
            pltpu.VMEM((2, SPAN, 2 * ROPE), BF16),
            pltpu.VMEM((4, ROWS, 2 * ROPE), BF16),
            pltpu.VMEM((ROWS, ROWS), BF16),
            pltpu.VMEM((ROWS, ROWS), BF16),
            pltpu.VMEM((GROUPS, N_CTX, 2 * SLOT, NOPE), BF16),
            pltpu.VMEM((GROUPS, N_CTX, 2 * SLOT, NOPE), BF16),
            pltpu.VMEM((N_CTX, SLOT, 128), jnp.int32),
            pltpu.VMEM((N_CTX, SLOT, 128), jnp.int32),
            dma((5,)),
            dma,
            dma((3,)),
            dma((5,)),
            dma((2,)),
            dma,
            dma,
            dma((GROUPS,)),
            dma((GROUPS,)),
        ],
        compiler_params=pltpu.CompilerParams(
            collective_id=0, has_side_effects=True, vmem_limit_bytes=62 << 20
        ),
        name="attend_and_place",
    )(query_nope, query_rope, latent, key_up, value_up, doc_lengths, owner.reshape(1, ROWS))


def solution(mesh):
    in_specs = (
        P("ctx", "head"),
        P("ctx", "head"),
        P(("ctx", "head"), None),
        P(None, "head"),
        P(None, "head"),
        P(),
        P("ctx"),
    )
    return jax.shard_map(
        per_device, mesh=mesh, in_specs=in_specs, out_specs=P("ctx", "head"), check_vma=False
    )
```

```python
import functools

import jax
import jax.numpy as jnp
from jax import lax
from jax.experimental import pallas as pl
from jax.experimental.pallas import tpu as pltpu
from jax.sharding import PartitionSpec as P

LATENT = 512
ROPE = 64
NOPE = 128
ROWS = 256
N_CTX = 32
N_HEAD = 8
HALF = 16
BLOCKS = 5
SPAN = BLOCKS * ROWS
HALF_SPAN = SPAN // 2
WINDOW = 1024
GROUPS = 8
SLOT = 8
DOCS = 8
FAR = -1e30
TO_EXP2 = 1.4426950408889634 / float(NOPE + ROPE) ** 0.5
FAR_FIRST = sorted(range(1, N_CTX), key=lambda ahead: abs(ahead - N_CTX // 2))
MESH = pl.DeviceIdType.MESH
F32 = jnp.float32
BF16 = jnp.bfloat16


def iota(shape, dim):
    return lax.broadcasted_iota(jnp.int32, shape, dim)


def kernel(
    qn_hbm, qr_hbm, lat_hbm, ku_hbm, vu_hbm, docs_hbm, owner_hbm, out_ref,
    docs, owner_ref, qn, qr, ku, vu, buf, kr, qbits, perm, place, outb, inb, idx_out, idx_in,
    load_sem, lat_sem, x_send, y_send, row_send, pair_send, x_recv, y_recv, row_recv, pair_recv,
    fsend, frecv, isend, irecv, asend, arecv, near_sem, far_sem,
):
    c = lax.axis_index("ctx")
    h = lax.axis_index("head")
    k = jnp.bitwise_and(c, 1)
    x = h // 2
    yh = jnp.bitwise_and(h, 1)
    sibling = (c + 1 - 2 * k, h)

    def at(ahead):
        return (jnp.bitwise_and(c + ahead + N_CTX, N_CTX - 1), h)

    def across(ahead, flip):
        return (jnp.bitwise_and(c + ahead + N_CTX, N_CTX - 1), 2 * x + yh + flip - 2 * yh * flip)

    def along(j):
        return (c, 2 * jnp.bitwise_and(x + j, 3) + yh)

    def remote(src, dst, send, recv, to):
        return pltpu.make_async_remote_copy(
            src, dst, send, recv, device_id=to, device_id_type=MESH
        )

    def wait(ref, sem):
        pltpu.make_async_copy(ref, ref, sem).wait()

    own_row = buf.at[0, 4, pl.ds(4 * yh, 4)]
    own_a = buf.at[0, 4, 4 * yh + x]
    own_b = buf.at[1, 4, h]
    lat_in = [
        pltpu.make_async_copy(lat_hbm.at[pl.ds(HALF * i, HALF)], dst, lat_sem.at[i])
        for i, dst in enumerate((own_a, own_b))
    ]
    loads = [
        pltpu.make_async_copy(src, dst, load_sem.at[i])
        for i, (src, dst) in enumerate(
            (
                (owner_hbm, owner_ref), (docs_hbm, docs), (ku_hbm, ku), (vu_hbm, vu),
                (qn_hbm, qn), (qr_hbm, qr),
            )
        )
    ]
    for load in lat_in + loads:
        load.start()

    barrier = pltpu.get_barrier_semaphore()
    met = 0
    for plane in (0, -4, 4):
        for j in range(4):
            if plane or j:
                to = jnp.bitwise_and(c + plane + N_CTX, N_CTX - 4) + jnp.bitwise_and(c + j, 3)
                pl.semaphore_signal(barrier, inc=1, device_id=(to, h), device_id_type=MESH)
                met += 1
    for j in (1, 2, 3):
        pl.semaphore_signal(barrier, inc=1, device_id=along(j), device_id_type=MESH)
        met += 1
    for ahead in (0, 2, -2, 4, -4):
        pl.semaphore_signal(barrier, inc=1, device_id=across(ahead, 1), device_id_type=MESH)
        met += 1
    pl.semaphore_wait(barrier, met)
    for ahead in (4, -4):
        pl.semaphore_signal(near_sem, inc=1, device_id=at(ahead), device_id_type=MESH)

    for load in lat_in:
        load.wait()
    targets = [
        (n, ahead, slot, flip)
        for n, (ahead, slot, flip) in enumerate(
            ((2, 2, 0), (2, 2, 1), (4, 0, 0), (4, 0, 1), (0, 4, 1))
        )
    ]
    for n, ahead, slot, flip in targets:
        remote(own_b, buf.at[1, slot, h], y_send.at[n], y_recv.at[slot], across(ahead, flip)).start()
    for j in (1, 3, 2):
        remote(own_a, own_a, x_send.at[j - 1], x_recv, along(j)).start()

    wait(buf.at[0, 4, pl.ds(0, 3)], x_recv)
    for n, ahead, slot, flip in targets:
        remote(
            own_row, buf.at[0, slot, pl.ds(4 * yh, 4)], row_send.at[n], row_recv.at[slot],
            across(ahead, flip),
        ).start()
    for n, (slot, came) in enumerate(((2, 2), (4, 1), (0, 2))):
        wait(buf.at[1, slot, pl.ds(0, came)], y_recv.at[slot])
        pair = buf.at[1, slot, pl.ds(2 * x, 2)]
        for j in (1, 3, 2):
            remote(pair, pair, pair_send.at[3 * n + j - 1], pair_recv.at[slot], along(j)).start()

    pl.semaphore_wait(near_sem, 2)
    for ahead in (8, -8):
        pl.semaphore_signal(far_sem, inc=1, device_id=at(ahead), device_id_type=MESH)
    for load in loads[:2]:
        load.wait()
    owner = owner_ref[...]
    row = lax.shift_right_logical(owner, 8)
    place_row = jnp.bitwise_and(owner, ROWS - 1)
    step_row = jnp.bitwise_and(row - c + (2 * N_CTX - 1), N_CTX - 1)
    step_all = jnp.broadcast_to(step_row, (ROWS, ROWS))
    sub = iota((ROWS, ROWS), 0)
    lane = iota((ROWS, ROWS), 1)
    step_col = jnp.sum(jnp.where(sub == lane, step_all, 0), axis=1, keepdims=True)
    same = (step_col == step_row) & (sub < lane)
    rank = jnp.sum(jnp.where(same, 1, 0), axis=0, keepdims=True)
    slot_row = step_row * SLOT + rank
    hit = sub == slot_row
    perm[...] = jnp.where(hit, 1.0, 0.0).astype(BF16)
    place_col = jnp.sum(jnp.where(hit, place_row, 0), axis=1, keepdims=True)
    idx = jnp.broadcast_to(place_col, (ROWS, 128)).reshape(N_CTX, SLOT, 128)
    idx_out[...] = idx
    idx_in[N_CTX - 1] = idx[N_CTX - 1]

    lanes = iota((1, ROPE), 1)
    starts = jnp.zeros((1, ROPE), jnp.int32)
    ends = jnp.zeros((1, ROPE), jnp.int32)
    total = 0
    for d in range(DOCS):
        starts = jnp.where(lanes == d, total, starts)
        total = total + docs[d]
        ends = jnp.where(lanes == d, total, ends)
    step16 = iota((HALF_SPAN, ROPE), 0)
    within = jnp.bitwise_and(step16, 15)
    tile = jnp.bitwise_and(lax.shift_right_logical(step16, 4), 7)
    offset_a = jnp.bitwise_and(tile, 3) * 64 + lax.shift_right_logical(tile, 2) * 32 + within
    offset_b = tile * 32 + HALF + within
    block_pos = (c - 4 + lax.shift_right_logical(step16, 7)) * ROWS
    key_bits = []
    for offset in (offset_a, offset_b):
        key_pos = block_pos + offset
        key_in = (key_pos >= starts) & (key_pos < ends)
        key_bits.append(
            jnp.where(key_in | (iota((HALF_SPAN, ROPE), 1) >= DOCS), 0.0, 1.0).astype(BF16)
        )
    query_pos = c * ROWS + iota((ROWS, ROPE), 0)
    query_in = (query_pos >= starts) & (query_pos < ends)
    query_bits = jnp.where(query_in, FAR, 0.0)
    zeros = jnp.zeros((ROWS, ROPE), F32)
    ones = jnp.ones((ROWS, ROPE), F32)
    qbits[0] = jnp.concatenate([zeros, query_bits], axis=1).astype(BF16)
    qbits[1] = jnp.concatenate([query_bits, zeros], axis=1).astype(BF16)
    qbits[2] = jnp.concatenate([ones, zeros], axis=1).astype(BF16)
    qbits[3] = jnp.concatenate([zeros, ones], axis=1).astype(BF16)

    def forward(half, src, dst, n):
        remote(buf.at[half, src], buf.at[half, dst], fsend.at[n], frecv.at[n], sibling).start()

    wait(buf.at[0, 2], row_recv.at[2])
    forward(0, 2, 2 * k + 1, 0)
    wait(buf.at[1, 2, pl.ds(0, 6)], pair_recv.at[2])
    forward(1, 2, 2 * k + 1, 1)
    wait(buf.at[0, 4, pl.ds(0, 4)], row_recv.at[4])
    wait(buf.at[0, 0], row_recv.at[0])
    forward(0, 4 - 4 * k, 3 - 2 * k, 2)
    wait(buf.at[1, 4, pl.ds(0, 6)], pair_recv.at[4])
    wait(buf.at[1, 0, pl.ds(0, 6)], pair_recv.at[0])
    forward(1, 4 - 4 * k, 3 - 2 * k, 3)
    for n in range(4):
        wait(buf.at[0, 0], frecv.at[n])
    for load in loads[2:]:
        load.wait()

    for half in range(2):
        keys_here = pl.ds(half * HALF_SPAN, HALF_SPAN)
        rope = buf[half, :, :, :, LATENT:].reshape(HALF_SPAN, ROPE)
        kr[0, keys_here] = jnp.concatenate([rope, key_bits[half]], axis=1)
        kr[1, keys_here] = jnp.concatenate([key_bits[half], rope], axis=1)

    query_row = iota((ROWS, 128), 0)
    key_lane = iota((ROWS, 128), 1)
    within = jnp.bitwise_and(key_lane, 15)
    tile = lax.shift_right_logical(key_lane, 4)
    lower = [
        jnp.bitwise_and(tile, 3) * 64 + lax.shift_right_logical(tile, 2) * 32 + within <= query_row,
        tile * 32 + HALF + within <= query_row,
    ]

    def attend(g, carry):
        cols = pl.ds(pl.multiple_of(g * 2 * NOPE, 2 * NOPE), 2 * NOPE)
        latent = buf[:, :, :, :, :LATENT].reshape(SPAN, LATENT)
        keys = jnp.dot(latent, ku[:, cols], preferred_element_type=F32).astype(BF16)
        values = jnp.dot(latent, vu[:, cols], preferred_element_type=F32).astype(BF16)
        q_two = qn[:, cols]
        r_two = qr[:, pl.ds(pl.multiple_of(g * 2 * ROPE, 2 * ROPE), 2 * ROPE)]
        outs = []
        for e in range(2):
            part = slice(e * NOPE, (e + 1) * NOPE)
            kx = jnp.concatenate([keys[:, part], kr[e]], axis=1)
            qx = jnp.concatenate([q_two[:, part], r_two * qbits[2 + e] + qbits[e]], axis=1)
            s = lax.dot_general(qx, kx, (((1,), (1,)), ((), ())), preferred_element_type=F32)
            parts = []
            for half in range(2):
                first = half * HALF_SPAN
                parts += [
                    jnp.where(lower[half], FAR, s[:, first : first + 128]),
                    s[:, first + 128 : first + 512],
                    jnp.where(lower[half], s[:, first + 512 : first + 640], FAR),
                ]
            s = jnp.concatenate(parts, axis=1)
            largest = jnp.max(s, axis=1, keepdims=True)
            p = jnp.exp2((s - largest) * TO_EXP2)
            weight = jnp.sum(p, axis=1, keepdims=True)
            o = jnp.dot(p.astype(BF16), values[:, part], preferred_element_type=F32)
            outs.append((o / weight).astype(BF16))
        both = jnp.concatenate(outs, axis=1)
        sorted_ = jnp.dot(perm[...], both, preferred_element_type=F32)
        sorted_ = sorted_.reshape(N_CTX, SLOT, 2 * NOPE)
        packed = jnp.concatenate([sorted_[:, :, :NOPE], sorted_[:, :, NOPE:]], axis=1).astype(BF16)
        outb[g] = packed
        inb[g, N_CTX - 1] = packed[N_CTX - 1]

        @pl.when(g == 0)
        def first_sends():
            pl.semaphore_wait(far_sem, 2)
            for ahead in FAR_FIRST:
                remote(
                    idx_out.at[ahead - 1], idx_in.at[ahead - 1], isend, irecv, at(ahead)
                ).start()

        for ahead in FAR_FIRST:
            remote(
                outb.at[g, ahead - 1], inb.at[g, ahead - 1], asend.at[g], arecv.at[g], at(ahead)
            ).start()
        return carry

    lax.fori_loop(0, GROUPS, attend, 0)

    rest = pl.ds(0, N_CTX - 1)
    wait(idx_in.at[rest], irecv)
    goal = idx_in[...].reshape(ROWS, 128)
    goal = jnp.concatenate([goal, goal], axis=1)
    place[...] = jnp.where(goal == lane, 1.0, 0.0).T.astype(BF16)

    def settle(g, carry):
        cols = pl.ds(pl.multiple_of(g * 2 * NOPE, 2 * NOPE), 2 * NOPE)
        wait(inb.at[g, rest], arecv.at[g])
        got = inb[g].astype(F32)
        got = jnp.concatenate([got[:, :SLOT], got[:, SLOT:]], axis=2).reshape(ROWS, 2 * NOPE)
        out_ref[:, cols] = jnp.dot(
            place[...], got.astype(BF16), preferred_element_type=F32
        ).astype(BF16)
        return carry

    lax.fori_loop(0, GROUPS, settle, 0)

    for n in range(3):
        wait(own_a, x_send.at[n])
    for n in range(5):
        wait(own_b, y_send.at[n])
        wait(own_row, row_send.at[n])
    for n in range(9):
        wait(buf.at[1, 0, pl.ds(0, 2)], pair_send.at[n])
    for n in range(4):
        wait(buf.at[0, 0], fsend.at[n])
    wait(idx_out.at[rest], isend)

    def all_sent(g, carry):
        wait(outb.at[g, rest], asend.at[g])
        return carry

    lax.fori_loop(0, GROUPS, all_sent, 0)


def per_device(query_nope, query_rope, latent, key_up, value_up, doc_lengths, owner):
    hbm = pl.BlockSpec(memory_space=pltpu.HBM)
    dma = pltpu.SemaphoreType.DMA
    regular = pltpu.SemaphoreType.REGULAR
    args = (query_nope, query_rope, latent, key_up, value_up, doc_lengths, owner.reshape(1, ROWS))
    return pl.pallas_call(
        kernel,
        out_shape=pltpu.VMEM(query_nope.shape, BF16),
        in_specs=[hbm] * len(args),
        out_specs=pl.BlockSpec(memory_space=pltpu.VMEM),
        scratch_shapes=[
            pltpu.SMEM((DOCS,), jnp.int32),
            pltpu.VMEM((1, ROWS), jnp.int32),
            pltpu.VMEM(query_nope.shape, BF16),
            pltpu.VMEM(query_rope.shape, BF16),
            pltpu.VMEM(key_up.shape, BF16),
            pltpu.VMEM(value_up.shape, BF16),
            pltpu.VMEM((2, BLOCKS, N_HEAD, HALF, LATENT + ROPE), BF16),
            pltpu.VMEM((2, SPAN, 2 * ROPE), BF16),
            pltpu.VMEM((4, ROWS, 2 * ROPE), BF16),
            pltpu.VMEM((ROWS, ROWS), BF16),
            pltpu.VMEM((ROWS, ROWS), BF16),
            pltpu.VMEM((GROUPS, N_CTX, 2 * SLOT, NOPE), BF16),
            pltpu.VMEM((GROUPS, N_CTX, 2 * SLOT, NOPE), BF16),
            pltpu.VMEM((N_CTX, SLOT, 128), jnp.int32),
            pltpu.VMEM((N_CTX, SLOT, 128), jnp.int32),
            dma((6,)),
            dma((2,)),
            dma((3,)),
            dma((5,)),
            dma((5,)),
            dma((9,)),
            dma,
            dma((5,)),
            dma((5,)),
            dma((5,)),
            dma((4,)),
            dma((4,)),
            dma,
            dma,
            dma((GROUPS,)),
            dma((GROUPS,)),
            regular,
            regular,
        ],
        compiler_params=pltpu.CompilerParams(
            collective_id=0, has_side_effects=True, vmem_limit_bytes=48 << 20
        ),
        name="attend_and_place",
    )(*[pltpu.with_memory_space_constraint(a, pltpu.HBM) for a in args])


def solution(mesh):
    in_specs = (
        P("ctx", "head"),
        P("ctx", "head"),
        P(("ctx", "head"), None),
        P(None, "head"),
        P(None, "head"),
        P(),
        P("ctx"),
    )
    return jax.shard_map(
        per_device, mesh=mesh, in_specs=in_specs, out_specs=P("ctx", "head"), check_vma=False
    )
```

```python
import functools

import jax
import jax.numpy as jnp
from jax import lax
from jax.experimental import pallas as pl
from jax.experimental.pallas import tpu as pltpu
from jax.sharding import PartitionSpec as P

LATENT = 512
ROPE = 64
NOPE = 128
ROWS = 256
N_CTX = 32
N_HEAD = 8
HALF = 16
BLOCKS = 5
SPAN = BLOCKS * ROWS
HALF_SPAN = SPAN // 2
WINDOW = 1024
GROUPS = 8
SLOT = 8
DOCS = 8
FAR = -1e30
TO_EXP2 = 1.4426950408889634 / float(NOPE + ROPE) ** 0.5
FAR_FIRST = sorted(range(1, N_CTX), key=lambda ahead: abs(ahead - N_CTX // 2))
MESH = pl.DeviceIdType.MESH
F32 = jnp.float32
BF16 = jnp.bfloat16


def iota(shape, dim):
    return lax.broadcasted_iota(jnp.int32, shape, dim)


def kernel(
    qn_hbm, qr_hbm, lat_hbm, ku_hbm, vu_hbm, docs_hbm, owner_hbm, out_ref,
    docs, owner_ref, qn, qr, ku, vu, buf, kr, qbits, perm, place, outb, inb, idx_out, idx_in,
    load_sem, lat_sem, x_send, y_send, row_send, pair_send, x_recv, y_recv, row_recv, pair_recv,
    fsend, frecv, isend, irecv, asend, arecv, near_sem, far_sem,
):
    c = lax.axis_index("ctx")
    h = lax.axis_index("head")
    k = jnp.bitwise_and(c, 1)
    x = h // 2
    yh = jnp.bitwise_and(h, 1)
    sibling = (c + 1 - 2 * k, h)

    def at(ahead):
        return (jnp.bitwise_and(c + ahead + N_CTX, N_CTX - 1), h)

    def across(ahead, flip):
        return (jnp.bitwise_and(c + ahead + N_CTX, N_CTX - 1), 2 * x + yh + flip - 2 * yh * flip)

    def along(j):
        return (c, 2 * jnp.bitwise_and(x + j, 3) + yh)

    def remote(src, dst, send, recv, to):
        return pltpu.make_async_remote_copy(
            src, dst, send, recv, device_id=to, device_id_type=MESH
        )

    def wait(ref, sem):
        pltpu.make_async_copy(ref, ref, sem).wait()

    own_a = buf.at[0, 4, 4 * yh + x]
    own_b = buf.at[1, 4, h]
    lat_in = [
        pltpu.make_async_copy(lat_hbm.at[pl.ds(HALF * i, HALF)], dst, lat_sem.at[i])
        for i, dst in enumerate((own_a, own_b))
    ]
    loads = [
        pltpu.make_async_copy(src, dst, load_sem.at[i])
        for i, (src, dst) in enumerate(
            (
                (owner_hbm, owner_ref), (docs_hbm, docs), (ku_hbm, ku), (vu_hbm, vu),
                (qn_hbm, qn), (qr_hbm, qr),
            )
        )
    ]
    for load in lat_in + loads:
        load.start()

    barrier = pltpu.get_barrier_semaphore()
    met = 0
    for plane in (0, -4, 4):
        for j in range(4):
            if plane or j:
                to = jnp.bitwise_and(c + plane + N_CTX, N_CTX - 4) + jnp.bitwise_and(c + j, 3)
                pl.semaphore_signal(barrier, inc=1, device_id=(to, h), device_id_type=MESH)
                met += 1
    for j in (1, 2, 3):
        pl.semaphore_signal(barrier, inc=1, device_id=along(j), device_id_type=MESH)
        met += 1
    for ahead in (0, 2, -2, 4, -4):
        pl.semaphore_signal(barrier, inc=1, device_id=across(ahead, 1), device_id_type=MESH)
        met += 1
    pl.semaphore_wait(barrier, met)
    for ahead in (4, -4):
        pl.semaphore_signal(near_sem, inc=1, device_id=at(ahead), device_id_type=MESH)

    for load in lat_in:
        load.wait()
    targets = [
        (n, ahead, slot, flip)
        for n, (ahead, slot, flip) in enumerate(
            ((2, 2, 0), (2, 2, 1), (4, 0, 0), (4, 0, 1), (0, 4, 1))
        )
    ]
    for j in (1, 3, 2):
        remote(own_a, own_a, x_send.at[j - 1], x_recv.at[j - 1], along(j)).start()
    for n, ahead, slot, flip in targets:
        remote(own_b, buf.at[1, slot, h], y_send.at[n], y_recv.at[n], across(ahead, flip)).start()

    def send_row(j):
        from_x = 4 * yh + jnp.bitwise_and(x - j, 3)
        if j:
            wait(own_a, x_recv.at[j - 1])
        for n, ahead, slot, flip in targets:
            remote(
                buf.at[0, 4, from_x], buf.at[0, slot, from_x], row_send.at[5 * j + n],
                row_recv.at[slot], across(ahead, flip),
            ).start()

    def send_pair(n, slot, flip):
        from_y = 2 * x + yh + flip - 2 * yh * flip
        if n < 5:
            wait(own_b, y_recv.at[n])
        piece = buf.at[1, slot, from_y]
        for j in (1, 3, 2):
            remote(piece, piece, pair_send.at[3 * n + j - 1], pair_recv.at[slot], along(j)).start()

    send_row(0)
    send_pair(5, 4, 0)
    send_row(1)
    send_row(3)
    send_pair(0, 2, 0)
    send_pair(1, 2, 1)
    send_pair(2, 0, 0)
    send_pair(4, 4, 1)
    send_row(2)
    send_pair(3, 0, 1)

    pl.semaphore_wait(near_sem, 2)
    for ahead in (8, -8):
        pl.semaphore_signal(far_sem, inc=1, device_id=at(ahead), device_id_type=MESH)
    for load in loads[:2]:
        load.wait()
    owner = owner_ref[...]
    row = lax.shift_right_logical(owner, 8)
    place_row = jnp.bitwise_and(owner, ROWS - 1)
    step_row = jnp.bitwise_and(row - c + (2 * N_CTX - 1), N_CTX - 1)
    step_all = jnp.broadcast_to(step_row, (ROWS, ROWS))
    sub = iota((ROWS, ROWS), 0)
    lane = iota((ROWS, ROWS), 1)
    step_col = jnp.sum(jnp.where(sub == lane, step_all, 0), axis=1, keepdims=True)
    same = (step_col == step_row) & (sub < lane)
    rank = jnp.sum(jnp.where(same, 1, 0), axis=0, keepdims=True)
    slot_row = step_row * SLOT + rank
    hit = sub == slot_row
    perm[...] = jnp.where(hit, 1.0, 0.0).astype(BF16)
    place_col = jnp.sum(jnp.where(hit, place_row, 0), axis=1, keepdims=True)
    place_slot = jnp.sum(jnp.where(sub == lane, place_col, 0), axis=0, keepdims=True)
    half_sub = iota((N_CTX // 2, 128), 0)
    half_lane = lax.shift_right_logical(iota((N_CTX // 2, 128), 1), 3)
    for part in range(2):
        spread = jnp.where(
            half_sub == half_lane, place_slot[:, part * 128 : (part + 1) * 128], 0
        )
        for j in range(N_CTX // 2):
            idx_out[part * N_CTX // 2 + j] = spread[j : j + 1]
    idx_in[N_CTX - 1] = idx_out[N_CTX - 1]

    lanes = iota((1, ROPE), 1)
    starts = jnp.zeros((1, ROPE), jnp.int32)
    ends = jnp.zeros((1, ROPE), jnp.int32)
    total = 0
    for d in range(DOCS):
        starts = jnp.where(lanes == d, total, starts)
        total = total + docs[d]
        ends = jnp.where(lanes == d, total, ends)
    step16 = iota((HALF_SPAN, ROPE), 0)
    within = jnp.bitwise_and(step16, 15)
    tile = jnp.bitwise_and(lax.shift_right_logical(step16, 4), 7)
    offset_a = jnp.bitwise_and(tile, 3) * 64 + lax.shift_right_logical(tile, 2) * 32 + within
    offset_b = tile * 32 + HALF + within
    block_pos = (c - 4 + lax.shift_right_logical(step16, 7)) * ROWS
    key_bits = []
    for offset in (offset_a, offset_b):
        key_pos = block_pos + offset
        key_in = (key_pos >= starts) & (key_pos < ends)
        key_bits.append(
            jnp.where(key_in | (iota((HALF_SPAN, ROPE), 1) >= DOCS), 0.0, 1.0).astype(BF16)
        )
    query_pos = c * ROWS + iota((ROWS, ROPE), 0)
    query_in = (query_pos >= starts) & (query_pos < ends)
    query_bits = jnp.where(query_in, FAR, 0.0)
    zeros = jnp.zeros((ROWS, ROPE), F32)
    ones = jnp.ones((ROWS, ROPE), F32)
    qbits[0] = jnp.concatenate([zeros, query_bits], axis=1).astype(BF16)
    qbits[1] = jnp.concatenate([query_bits, zeros], axis=1).astype(BF16)
    qbits[2] = jnp.concatenate([ones, zeros], axis=1).astype(BF16)
    qbits[3] = jnp.concatenate([zeros, ones], axis=1).astype(BF16)

    def forward(half, src, dst, n):
        remote(buf.at[half, src], buf.at[half, dst], fsend.at[n], frecv.at[n], sibling).start()

    wait(buf.at[0, 2], row_recv.at[2])
    forward(0, 2, 2 * k + 1, 0)
    wait(buf.at[1, 2, pl.ds(0, 6)], pair_recv.at[2])
    forward(1, 2, 2 * k + 1, 1)
    wait(buf.at[0, 4, pl.ds(0, 4)], row_recv.at[4])
    wait(buf.at[0, 0], row_recv.at[0])
    forward(0, 4 - 4 * k, 3 - 2 * k, 2)
    wait(buf.at[1, 4, pl.ds(0, 6)], pair_recv.at[4])
    wait(buf.at[1, 0, pl.ds(0, 6)], pair_recv.at[0])
    forward(1, 4 - 4 * k, 3 - 2 * k, 3)
    for n in range(4):
        wait(buf.at[0, 0], frecv.at[n])
    for load in loads[2:]:
        load.wait()

    for half in range(2):
        keys_here = pl.ds(half * HALF_SPAN, HALF_SPAN)
        rope = buf[half, :, :, :, LATENT:].reshape(HALF_SPAN, ROPE)
        kr[0, keys_here] = jnp.concatenate([rope, key_bits[half]], axis=1)
        kr[1, keys_here] = jnp.concatenate([key_bits[half], rope], axis=1)

    query_row = iota((ROWS, 128), 0)
    key_lane = iota((ROWS, 128), 1)
    within = jnp.bitwise_and(key_lane, 15)
    tile = lax.shift_right_logical(key_lane, 4)
    lower = [
        jnp.bitwise_and(tile, 3) * 64 + lax.shift_right_logical(tile, 2) * 32 + within <= query_row,
        tile * 32 + HALF + within <= query_row,
    ]

    def attend(g, carry):
        cols = pl.ds(pl.multiple_of(g * 2 * NOPE, 2 * NOPE), 2 * NOPE)
        latent = buf[:, :, :, :, :LATENT].reshape(SPAN, LATENT)
        keys = jnp.dot(latent, ku[:, cols], preferred_element_type=F32).astype(BF16)
        values = jnp.dot(latent, vu[:, cols], preferred_element_type=F32).astype(BF16)
        q_two = qn[:, cols]
        r_two = qr[:, pl.ds(pl.multiple_of(g * 2 * ROPE, 2 * ROPE), 2 * ROPE)]
        outs = []
        for e in range(2):
            part = slice(e * NOPE, (e + 1) * NOPE)
            kx = jnp.concatenate([keys[:, part], kr[e]], axis=1)
            qx = jnp.concatenate([q_two[:, part], r_two * qbits[2 + e] + qbits[e]], axis=1)
            s = lax.dot_general(qx, kx, (((1,), (1,)), ((), ())), preferred_element_type=F32)
            parts = []
            for half in range(2):
                first = half * HALF_SPAN
                parts += [
                    jnp.where(lower[half], FAR, s[:, first : first + 128]),
                    s[:, first + 128 : first + 512],
                    jnp.where(lower[half], s[:, first + 512 : first + 640], FAR),
                ]
            s = jnp.concatenate(parts, axis=1)
            largest = jnp.max(s, axis=1, keepdims=True)
            p = jnp.exp2((s - largest) * TO_EXP2)
            weight = jnp.sum(p, axis=1, keepdims=True)
            o = jnp.dot(p.astype(BF16), values[:, part], preferred_element_type=F32)
            outs.append((o / weight).astype(BF16))
        both = jnp.concatenate(outs, axis=1)
        sorted_ = jnp.dot(perm[...], both, preferred_element_type=F32)
        sorted_ = sorted_.reshape(N_CTX, SLOT, 2 * NOPE)
        packed = jnp.concatenate([sorted_[:, :, :NOPE], sorted_[:, :, NOPE:]], axis=1).astype(BF16)
        outb[g] = packed
        inb[g, N_CTX - 1] = packed[N_CTX - 1]

        @pl.when(g == 0)
        def first_sends():
            pl.semaphore_wait(far_sem, 2)
            for ahead in FAR_FIRST:
                remote(
                    idx_out.at[ahead - 1], idx_in.at[ahead - 1], isend, irecv, at(ahead)
                ).start()

        for ahead in FAR_FIRST:
            remote(
                outb.at[g, ahead - 1], inb.at[g, ahead - 1], asend.at[g], arecv.at[g], at(ahead)
            ).start()
        return carry

    lax.fori_loop(0, GROUPS, attend, 0)

    rest = pl.ds(0, N_CTX - 1)
    wait(idx_in.at[rest], irecv)
    goals = []
    for part in range(2):
        goal = idx_in[part * N_CTX // 2]
        for j in range(1, N_CTX // 2):
            goal = goal + idx_in[part * N_CTX // 2 + j]
        goals.append(goal)
    place[...] = jnp.where(jnp.concatenate(goals, axis=1) == sub, 1.0, 0.0).astype(BF16)

    def settle(g, carry):
        cols = pl.ds(pl.multiple_of(g * 2 * NOPE, 2 * NOPE), 2 * NOPE)
        wait(inb.at[g, rest], arecv.at[g])
        got = inb[g].astype(F32)
        got = jnp.concatenate([got[:, :SLOT], got[:, SLOT:]], axis=2).reshape(ROWS, 2 * NOPE)
        out_ref[:, cols] = jnp.dot(
            place[...], got.astype(BF16), preferred_element_type=F32
        ).astype(BF16)
        return carry

    lax.fori_loop(0, GROUPS, settle, 0)

    for n in range(3):
        wait(own_a, x_send.at[n])
    for n in range(5):
        wait(own_b, y_send.at[n])
    for n in range(20):
        wait(own_a, row_send.at[n])
    for n in range(18):
        wait(own_b, pair_send.at[n])
    for n in range(4):
        wait(buf.at[0, 0], fsend.at[n])
    wait(idx_out.at[rest], isend)

    def all_sent(g, carry):
        wait(outb.at[g, rest], asend.at[g])
        return carry

    lax.fori_loop(0, GROUPS, all_sent, 0)


def per_device(query_nope, query_rope, latent, key_up, value_up, doc_lengths, owner):
    hbm = pl.BlockSpec(memory_space=pltpu.HBM)
    dma = pltpu.SemaphoreType.DMA
    regular = pltpu.SemaphoreType.REGULAR
    args = (query_nope, query_rope, latent, key_up, value_up, doc_lengths, owner.reshape(1, ROWS))
    return pl.pallas_call(
        kernel,
        out_shape=pltpu.VMEM(query_nope.shape, BF16),
        in_specs=[hbm] * len(args),
        out_specs=pl.BlockSpec(memory_space=pltpu.VMEM),
        scratch_shapes=[
            pltpu.SMEM((DOCS,), jnp.int32),
            pltpu.VMEM((1, ROWS), jnp.int32),
            pltpu.VMEM(query_nope.shape, BF16),
            pltpu.VMEM(query_rope.shape, BF16),
            pltpu.VMEM(key_up.shape, BF16),
            pltpu.VMEM(value_up.shape, BF16),
            pltpu.VMEM((2, BLOCKS, N_HEAD, HALF, LATENT + ROPE), BF16),
            pltpu.VMEM((2, SPAN, 2 * ROPE), BF16),
            pltpu.VMEM((4, ROWS, 2 * ROPE), BF16),
            pltpu.VMEM((ROWS, ROWS), BF16),
            pltpu.VMEM((ROWS, ROWS), BF16),
            pltpu.VMEM((GROUPS, N_CTX, 2 * SLOT, NOPE), BF16),
            pltpu.VMEM((GROUPS, N_CTX, 2 * SLOT, NOPE), BF16),
            pltpu.VMEM((N_CTX, 1, 128), jnp.int32),
            pltpu.VMEM((N_CTX, 1, 128), jnp.int32),
            dma((6,)),
            dma((2,)),
            dma((3,)),
            dma((5,)),
            dma((20,)),
            dma((18,)),
            dma((3,)),
            dma((5,)),
            dma((5,)),
            dma((5,)),
            dma((4,)),
            dma((4,)),
            dma,
            dma,
            dma((GROUPS,)),
            dma((GROUPS,)),
            regular,
            regular,
        ],
        compiler_params=pltpu.CompilerParams(
            collective_id=0, has_side_effects=True, vmem_limit_bytes=48 << 20
        ),
        name="attend_and_place",
    )(*[pltpu.with_memory_space_constraint(a, pltpu.HBM) for a in args])


def solution(mesh):
    in_specs = (
        P("ctx", "head"),
        P("ctx", "head"),
        P(("ctx", "head"), None),
        P(None, "head"),
        P(None, "head"),
        P(),
        P("ctx"),
    )
    return jax.shard_map(
        per_device, mesh=mesh, in_specs=in_specs, out_specs=P("ctx", "head"), check_vma=False
    )
```

```python
import functools

import jax
import jax.numpy as jnp
from jax import lax
from jax.experimental import pallas as pl
from jax.experimental.pallas import tpu as pltpu
from jax.sharding import PartitionSpec as P

LATENT = 512
ROPE = 64
NOPE = 128
ROWS = 256
N_CTX = 32
N_HEAD = 8
HALF = 16
BLOCKS = 5
SPAN = BLOCKS * ROWS
HALF_SPAN = SPAN // 2
WINDOW = 1024
GROUPS = 8
SLOT = 8
DOCS = 8
FAR = -1e30
TO_EXP2 = 1.4426950408889634 / float(NOPE + ROPE) ** 0.5
FAR_FIRST = sorted(range(1, N_CTX), key=lambda ahead: abs(ahead - N_CTX // 2))
MESH = pl.DeviceIdType.MESH
F32 = jnp.float32
BF16 = jnp.bfloat16


def iota(shape, dim):
    return lax.broadcasted_iota(jnp.int32, shape, dim)


def kernel(
    qn_hbm, qr_hbm, lat_hbm, ku_hbm, vu_hbm, docs_hbm, owner_hbm, out_ref,
    docs, owner_ref, qn, qr, ku, vu, stage, buf0, buf1, kv, kr, qbits, perm, place, outb, inb, idx_out, idx_in,
    load_sem, lat_sem, x_send, y_send, row_send, pair_send, x_recv, y_recv, row_recv, pair_recv,
    fsend, frecv, isend, irecv, asend, arecv, near_sem, far_sem,
):
    c = lax.axis_index("ctx")
    h = lax.axis_index("head")
    k = jnp.bitwise_and(c, 1)
    x = h // 2
    yh = jnp.bitwise_and(h, 1)
    sibling = (c + 1 - 2 * k, h)

    def at(ahead):
        return (jnp.bitwise_and(c + ahead + N_CTX, N_CTX - 1), h)

    def across(ahead, flip):
        return (jnp.bitwise_and(c + ahead + N_CTX, N_CTX - 1), 2 * x + yh + flip - 2 * yh * flip)

    def along(j):
        return (c, 2 * jnp.bitwise_and(x + j, 3) + yh)

    def remote(src, dst, send, recv, to):
        return pltpu.make_async_remote_copy(
            src, dst, send, recv, device_id=to, device_id_type=MESH
        )

    def wait(ref, sem):
        pltpu.make_async_copy(ref, ref, sem).wait()

    own_a = buf0.at[4, 4 * yh + x]
    own_b = buf1.at[4, h]
    lat_in = pltpu.make_async_copy(lat_hbm, stage, lat_sem)
    loads = [
        pltpu.make_async_copy(src, dst, load_sem.at[i])
        for i, (src, dst) in enumerate(
            (
                (owner_hbm, owner_ref), (docs_hbm, docs), (ku_hbm, ku), (vu_hbm, vu),
                (qn_hbm, qn), (qr_hbm, qr),
            )
        )
    ]
    for load in [lat_in] + loads:
        load.start()

    barrier = pltpu.get_barrier_semaphore()
    met = 0
    for plane in (0, -4, 4):
        for j in range(4):
            if plane or j:
                to = jnp.bitwise_and(c + plane + N_CTX, N_CTX - 4) + jnp.bitwise_and(c + j, 3)
                pl.semaphore_signal(barrier, inc=1, device_id=(to, h), device_id_type=MESH)
                met += 1
    for j in (1, 2, 3):
        pl.semaphore_signal(barrier, inc=1, device_id=along(j), device_id_type=MESH)
        met += 1
    for ahead in (0, 2, -2, 4, -4):
        pl.semaphore_signal(barrier, inc=1, device_id=across(ahead, 1), device_id_type=MESH)
        met += 1
    pl.semaphore_wait(barrier, met)
    for ahead in (4, -4):
        pl.semaphore_signal(near_sem, inc=1, device_id=at(ahead), device_id_type=MESH)

    lat_in.wait()
    rows = stage[...]
    buf0[4, 4 * yh + x] = rows[:HALF, :LATENT]
    buf1[4, h] = jnp.concatenate(
        [rows[HALF:, :LATENT], rows[:HALF, LATENT:], rows[HALF:, LATENT:]], axis=1
    )
    targets = [
        (n, ahead, slot, flip)
        for n, (ahead, slot, flip) in enumerate(
            ((2, 2, 0), (2, 2, 1), (4, 0, 0), (4, 0, 1), (0, 4, 1))
        )
    ]
    for j in (1, 3, 2):
        remote(own_a, own_a, x_send.at[j - 1], x_recv.at[j - 1], along(j)).start()
    for n, ahead, slot, flip in targets:
        remote(own_b, buf1.at[slot, h], y_send.at[n], y_recv.at[n], across(ahead, flip)).start()

    def send_row(j):
        from_x = 4 * yh + jnp.bitwise_and(x - j, 3)
        if j:
            wait(own_a, x_recv.at[j - 1])
        for n, ahead, slot, flip in targets:
            remote(
                buf0.at[4, from_x], buf0.at[slot, from_x], row_send.at[5 * j + n],
                row_recv.at[slot], across(ahead, flip),
            ).start()

    def send_pair(n, slot, flip):
        from_y = 2 * x + yh + flip - 2 * yh * flip
        if n < 5:
            wait(own_b, y_recv.at[n])
        piece = buf1.at[slot, from_y]
        for j in (1, 3, 2):
            remote(piece, piece, pair_send.at[3 * n + j - 1], pair_recv.at[slot], along(j)).start()

    send_row(0)
    send_pair(5, 4, 0)
    send_row(1)
    send_row(3)
    pl.semaphore_wait(near_sem, 2)
    for ahead in (8, -8):
        pl.semaphore_signal(far_sem, inc=1, device_id=at(ahead), device_id_type=MESH)
    send_pair(0, 2, 0)
    send_pair(1, 2, 1)
    send_pair(2, 0, 0)
    send_pair(4, 4, 1)
    send_row(2)
    send_pair(3, 0, 1)

    for load in loads[:2]:
        load.wait()
    owner = owner_ref[...]
    row = lax.shift_right_logical(owner, 8)
    place_row = jnp.bitwise_and(owner, ROWS - 1)
    step_row = jnp.bitwise_and(row - c + (2 * N_CTX - 1), N_CTX - 1)
    step_all = jnp.broadcast_to(step_row, (ROWS, ROWS))
    sub = iota((ROWS, ROWS), 0)
    lane = iota((ROWS, ROWS), 1)
    step_col = jnp.sum(jnp.where(sub == lane, step_all, 0), axis=1, keepdims=True)
    same = (step_col == step_row) & (sub < lane)
    rank = jnp.sum(jnp.where(same, 1, 0), axis=0, keepdims=True)
    slot_row = step_row * SLOT + rank
    hit = sub == slot_row
    perm[...] = jnp.where(hit, 1.0, 0.0).astype(BF16)
    place_col = jnp.sum(jnp.where(hit, place_row, 0), axis=1, keepdims=True)
    place_slot = jnp.sum(jnp.where(sub == lane, place_col, 0), axis=0, keepdims=True)
    half_sub = iota((N_CTX // 2, 128), 0)
    half_lane = lax.shift_right_logical(iota((N_CTX // 2, 128), 1), 3)
    for part in range(2):
        spread = jnp.where(
            half_sub == half_lane, place_slot[:, part * 128 : (part + 1) * 128], 0
        )
        for j in range(N_CTX // 2):
            idx_out[part * N_CTX // 2 + j] = spread[j : j + 1]
    idx_in[N_CTX - 1] = idx_out[N_CTX - 1]

    lanes = iota((1, ROPE), 1)
    starts = jnp.zeros((1, ROPE), jnp.int32)
    ends = jnp.zeros((1, ROPE), jnp.int32)
    total = 0
    for d in range(DOCS):
        starts = jnp.where(lanes == d, total, starts)
        total = total + docs[d]
        ends = jnp.where(lanes == d, total, ends)
    step16 = iota((HALF_SPAN, ROPE), 0)
    within = jnp.bitwise_and(step16, 15)
    tile = jnp.bitwise_and(lax.shift_right_logical(step16, 4), 7)
    offset_a = jnp.bitwise_and(tile, 3) * 64 + lax.shift_right_logical(tile, 2) * 32 + within
    offset_b = tile * 32 + HALF + within
    block_pos = (c - 4 + lax.shift_right_logical(step16, 7)) * ROWS
    key_bits = []
    for offset in (offset_a, offset_b):
        key_pos = block_pos + offset
        key_in = (key_pos >= starts) & (key_pos < ends)
        key_bits.append(
            jnp.where(key_in | (iota((HALF_SPAN, ROPE), 1) >= DOCS), 0.0, 1.0).astype(BF16)
        )
    query_pos = c * ROWS + iota((ROWS, ROPE), 0)
    query_in = (query_pos >= starts) & (query_pos < ends)
    query_bits = jnp.where(query_in, FAR, 0.0)
    zeros = jnp.zeros((ROWS, ROPE), F32)
    ones = jnp.ones((ROWS, ROPE), F32)
    qbits[0] = jnp.concatenate([zeros, query_bits], axis=1).astype(BF16)
    qbits[1] = jnp.concatenate([query_bits, zeros], axis=1).astype(BF16)
    qbits[2] = jnp.concatenate([ones, zeros], axis=1).astype(BF16)
    qbits[3] = jnp.concatenate([zeros, ones], axis=1).astype(BF16)

    def forward(buf, src, dst, n):
        remote(buf.at[src], buf.at[dst], fsend.at[n], frecv.at[n], sibling).start()

    def prepare(slot):
        latent = latents((slot,))
        cols = slice(0, 2 * NOPE)
        keys = jnp.dot(latent, ku[:, cols], preferred_element_type=F32).astype(BF16)
        values = jnp.dot(latent, vu[:, cols], preferred_element_type=F32).astype(BF16)
        rope = buf1[slot, :, :, LATENT:]
        for half in range(2):
            here = pl.ds(half * HALF_SPAN + slot * 128, 128)
            part = slice(half * 128, (half + 1) * 128)
            kv[0, 0, here] = keys[part]
            kv[0, 1, here] = values[part]
            if half == 0:
                rotary = jnp.concatenate([rope[n] for n in (0, 2, 4, 6, 1, 3, 5, 7)], axis=0)
            else:
                rotary = rope.reshape(128, 2 * ROPE)
            rotary = rotary[:, half * ROPE : (half + 1) * ROPE]
            bits = key_bits[half][slot * 128 : (slot + 1) * 128]
            kr[0, here] = jnp.concatenate([rotary, bits], axis=1)
            kr[1, here] = jnp.concatenate([bits, rotary], axis=1)

    def latents(slots):
        return jnp.concatenate(
            [buf0[s].reshape(128, LATENT) for s in slots]
            + [buf1[s, :, :, :LATENT].reshape(128, LATENT) for s in slots],
            axis=0,
        )

    wait(buf0.at[2], row_recv.at[2])
    forward(buf0, 2, 2 * k + 1, 0)
    wait(buf1.at[2, pl.ds(0, 6)], pair_recv.at[2])
    forward(buf1, 2, 2 * k + 1, 1)
    wait(buf0.at[4, pl.ds(0, 4)], row_recv.at[4])
    wait(buf0.at[0], row_recv.at[0])
    forward(buf0, 4 - 4 * k, 3 - 2 * k, 2)
    wait(buf1.at[4, pl.ds(0, 6)], pair_recv.at[4])
    wait(buf1.at[0, pl.ds(0, 6)], pair_recv.at[0])
    forward(buf1, 4 - 4 * k, 3 - 2 * k, 3)

    pl.semaphore_wait(far_sem, 2)
    for ahead in FAR_FIRST:
        remote(idx_out.at[ahead - 1], idx_in.at[ahead - 1], isend, irecv, at(ahead)).start()
    for load in loads[2:]:
        load.wait()
    for slot in (2, 4, 0):
        prepare(slot)
    for n in range(4):
        wait((buf0, buf1)[n % 2].at[0], frecv.at[n])
    for slot in (1, 3):
        prepare(slot)

    query_row = iota((ROWS, 128), 0)
    key_lane = iota((ROWS, 128), 1)
    within = jnp.bitwise_and(key_lane, 15)
    tile = lax.shift_right_logical(key_lane, 4)
    lower = [
        jnp.bitwise_and(tile, 3) * 64 + lax.shift_right_logical(tile, 2) * 32 + within <= query_row,
        tile * 32 + HALF + within <= query_row,
    ]

    def attend(g, carry):
        cols = pl.ds(pl.multiple_of(g * 2 * NOPE, 2 * NOPE), 2 * NOPE)
        now = jnp.bitwise_and(g, 1)
        keys = kv[now, 0]
        values = kv[now, 1]
        q_two = qn[:, cols]
        r_two = qr[:, pl.ds(pl.multiple_of(g * 2 * ROPE, 2 * ROPE), 2 * ROPE)]
        outs = []
        for e in range(2):
            part = slice(e * NOPE, (e + 1) * NOPE)
            kx = jnp.concatenate([keys[:, part], kr[e]], axis=1)
            qx = jnp.concatenate([q_two[:, part], r_two * qbits[2 + e] + qbits[e]], axis=1)
            s = lax.dot_general(qx, kx, (((1,), (1,)), ((), ())), preferred_element_type=F32)
            parts = []
            for half in range(2):
                first = half * HALF_SPAN
                parts += [
                    jnp.where(lower[half], FAR, s[:, first : first + 128]),
                    s[:, first + 128 : first + 512],
                    jnp.where(lower[half], s[:, first + 512 : first + 640], FAR),
                ]
            s = jnp.concatenate(parts, axis=1)
            largest = jnp.max(s, axis=1, keepdims=True)
            p = jnp.exp2((s - largest) * TO_EXP2)
            weight = jnp.sum(p, axis=1, keepdims=True)
            o = jnp.dot(p.astype(BF16), values[:, part], preferred_element_type=F32)
            outs.append((o / weight).astype(BF16))
        both = jnp.concatenate(outs, axis=1)
        sorted_ = jnp.dot(perm[...], both, preferred_element_type=F32)
        sorted_ = sorted_.reshape(N_CTX, SLOT, 2 * NOPE)
        packed = jnp.concatenate([sorted_[:, :, :NOPE], sorted_[:, :, NOPE:]], axis=1).astype(BF16)
        outb[g] = packed
        inb[g, N_CTX - 1] = packed[N_CTX - 1]

        def send(ahead):
            remote(
                outb.at[g, ahead - 1], inb.at[g, ahead - 1], asend.at[g], arecv.at[g], at(ahead)
            ).start()

        @pl.when(g < GROUPS - 1)
        def far_first():
            for ahead in FAR_FIRST:
                send(ahead)

        @pl.when(g == GROUPS - 1)
        def in_order():
            for to in range(N_CTX):

                @pl.when(c != to)
                def send_to(to=to):
                    send(jnp.bitwise_and(to - c, N_CTX - 1))

        following = jnp.minimum(g + 1, GROUPS - 1) * 2 * NOPE
        cols = pl.ds(pl.multiple_of(following, 2 * NOPE), 2 * NOPE)
        latent = latents(range(BLOCKS))
        keys = jnp.dot(latent, ku[:, cols], preferred_element_type=F32)
        kv[1 - now, 0] = keys.astype(BF16)
        values = jnp.dot(latent, vu[:, cols], preferred_element_type=F32)
        kv[1 - now, 1] = values.astype(BF16)
        return carry

    lax.fori_loop(0, GROUPS, attend, 0)

    rest = pl.ds(0, N_CTX - 1)
    wait(idx_in.at[rest], irecv)
    goals = []
    for part in range(2):
        goal = idx_in[part * N_CTX // 2]
        for j in range(1, N_CTX // 2):
            goal = goal + idx_in[part * N_CTX // 2 + j]
        goals.append(goal)
    place[...] = jnp.where(jnp.concatenate(goals, axis=1) == sub, 1.0, 0.0).astype(BF16)

    def settle(g, carry):
        cols = pl.ds(pl.multiple_of(g * 2 * NOPE, 2 * NOPE), 2 * NOPE)
        wait(inb.at[g, rest], arecv.at[g])
        got = inb[g].astype(F32)
        got = jnp.concatenate([got[:, :SLOT], got[:, SLOT:]], axis=2).reshape(ROWS, 2 * NOPE)
        out_ref[:, cols] = jnp.dot(
            place[...], got.astype(BF16), preferred_element_type=F32
        ).astype(BF16)
        return carry

    lax.fori_loop(0, GROUPS, settle, 0)

    for n in range(3):
        wait(own_a, x_send.at[n])
    for n in range(5):
        wait(own_b, y_send.at[n])
    for n in range(20):
        wait(own_a, row_send.at[n])
    for n in range(18):
        wait(own_b, pair_send.at[n])
    for n in range(4):
        wait((buf0, buf1)[n % 2].at[0], fsend.at[n])
    wait(idx_out.at[rest], isend)

    def all_sent(g, carry):
        wait(outb.at[g, rest], asend.at[g])
        return carry

    lax.fori_loop(0, GROUPS, all_sent, 0)


def per_device(query_nope, query_rope, latent, key_up, value_up, doc_lengths, owner):
    hbm = pl.BlockSpec(memory_space=pltpu.HBM)
    dma = pltpu.SemaphoreType.DMA
    regular = pltpu.SemaphoreType.REGULAR
    args = (query_nope, query_rope, latent, key_up, value_up, doc_lengths, owner.reshape(1, ROWS))
    return pl.pallas_call(
        kernel,
        out_shape=pltpu.VMEM(query_nope.shape, BF16),
        in_specs=[hbm] * len(args),
        out_specs=pl.BlockSpec(memory_space=pltpu.VMEM),
        scratch_shapes=[
            pltpu.SMEM((DOCS,), jnp.int32),
            pltpu.VMEM((1, ROWS), jnp.int32),
            pltpu.VMEM(query_nope.shape, BF16),
            pltpu.VMEM(query_rope.shape, BF16),
            pltpu.VMEM(key_up.shape, BF16),
            pltpu.VMEM(value_up.shape, BF16),
            pltpu.VMEM((2 * HALF, LATENT + ROPE), BF16),
            pltpu.VMEM((BLOCKS, N_HEAD, HALF, LATENT), BF16),
            pltpu.VMEM((BLOCKS, N_HEAD, HALF, LATENT + 2 * ROPE), BF16),
            pltpu.VMEM((2, 2, SPAN, 2 * NOPE), BF16),
            pltpu.VMEM((2, SPAN, 2 * ROPE), BF16),
            pltpu.VMEM((4, ROWS, 2 * ROPE), BF16),
            pltpu.VMEM((ROWS, ROWS), BF16),
            pltpu.VMEM((ROWS, ROWS), BF16),
            pltpu.VMEM((GROUPS, N_CTX, 2 * SLOT, NOPE), BF16),
            pltpu.VMEM((GROUPS, N_CTX, 2 * SLOT, NOPE), BF16),
            pltpu.VMEM((N_CTX, 1, 128), jnp.int32),
            pltpu.VMEM((N_CTX, 1, 128), jnp.int32),
            dma((6,)),
            dma,
            dma((3,)),
            dma((5,)),
            dma((20,)),
            dma((18,)),
            dma((3,)),
            dma((5,)),
            dma((5,)),
            dma((5,)),
            dma((4,)),
            dma((4,)),
            dma,
            dma,
            dma((GROUPS,)),
            dma((GROUPS,)),
            regular,
            regular,
        ],
        compiler_params=pltpu.CompilerParams(
            collective_id=0, has_side_effects=True, vmem_limit_bytes=48 << 20
        ),
        name="attend_and_place",
    )(*[pltpu.with_memory_space_constraint(a, pltpu.HBM) for a in args])


def solution(mesh):
    in_specs = (
        P("ctx", "head"),
        P("ctx", "head"),
        P(("ctx", "head"), None),
        P(None, "head"),
        P(None, "head"),
        P(),
        P("ctx"),
    )
    return jax.shard_map(
        per_device, mesh=mesh, in_specs=in_specs, out_specs=P("ctx", "head"), check_vma=False
    )
```

```python
import functools

import jax
import jax.numpy as jnp
from jax import lax
from jax.experimental import pallas as pl
from jax.experimental.pallas import tpu as pltpu
from jax.sharding import PartitionSpec as P

LATENT = 512
ROPE = 64
NOPE = 128
ROWS = 256
N_CTX = 32
N_HEAD = 8
HALF = 16
BLOCKS = 5
SPAN = BLOCKS * ROWS
HALF_SPAN = SPAN // 2
WINDOW = 1024
GROUPS = 8
SLOT = 8
DOCS = 8
FAR = -1e30
TO_EXP2 = 1.4426950408889634 / float(NOPE + ROPE) ** 0.5
FAR_FIRST = sorted(range(1, N_CTX), key=lambda ahead: abs(ahead - N_CTX // 2))
MESH = pl.DeviceIdType.MESH
F32 = jnp.float32
BF16 = jnp.bfloat16


def iota(shape, dim):
    return lax.broadcasted_iota(jnp.int32, shape, dim)


def kernel(
    qn_hbm, qr_hbm, lat_hbm, ku_hbm, vu_hbm, docs_hbm, owner_hbm, out_ref,
    docs, owner_ref, qn, qr, ku, vu, stage, buf0, buf1, kv, kr, kbits, qbits, perm, place, outb, inb, idx_out, idx_in,
    load_sem, lat_sem, x_send, y_send, row_send, pair_send, x_recv, y_recv, row_recv, pair_recv,
    fsend, frecv, isend, irecv, asend, arecv, near_sem, far_sem,
):
    c = lax.axis_index("ctx")
    h = lax.axis_index("head")
    k = jnp.bitwise_and(c, 1)
    x = h // 2
    yh = jnp.bitwise_and(h, 1)
    sibling = (c + 1 - 2 * k, h)

    def at(ahead):
        return (jnp.bitwise_and(c + ahead + N_CTX, N_CTX - 1), h)

    def across(ahead, flip):
        return (jnp.bitwise_and(c + ahead + N_CTX, N_CTX - 1), 2 * x + yh + flip - 2 * yh * flip)

    def along(j):
        return (c, 2 * jnp.bitwise_and(x + j, 3) + yh)

    def remote(src, dst, send, recv, to):
        return pltpu.make_async_remote_copy(
            src, dst, send, recv, device_id=to, device_id_type=MESH
        )

    def wait(ref, sem):
        pltpu.make_async_copy(ref, ref, sem).wait()

    own_a = buf0.at[4, 4 * yh + x]
    own_b = buf1.at[4, h]
    lat_in = pltpu.make_async_copy(lat_hbm, stage, lat_sem)
    loads = [
        pltpu.make_async_copy(src, dst, load_sem.at[i])
        for i, (src, dst) in enumerate(
            (
                (owner_hbm, owner_ref), (docs_hbm, docs), (ku_hbm, ku), (vu_hbm, vu),
                (qn_hbm, qn), (qr_hbm, qr),
            )
        )
    ]
    for load in [lat_in] + loads:
        load.start()

    barrier = pltpu.get_barrier_semaphore()
    met = 0
    for plane in (0, -4, 4):
        for j in range(4):
            if plane or j:
                to = jnp.bitwise_and(c + plane + N_CTX, N_CTX - 4) + jnp.bitwise_and(c + j, 3)
                pl.semaphore_signal(barrier, inc=1, device_id=(to, h), device_id_type=MESH)
                met += 1
    for j in (1, 2, 3):
        pl.semaphore_signal(barrier, inc=1, device_id=along(j), device_id_type=MESH)
        met += 1
    for ahead in (0, 2, -2, 4, -4):
        pl.semaphore_signal(barrier, inc=1, device_id=across(ahead, 1), device_id_type=MESH)
        met += 1
    pl.semaphore_wait(barrier, met)
    for ahead in (4, -4):
        pl.semaphore_signal(near_sem, inc=1, device_id=at(ahead), device_id_type=MESH)

    lat_in.wait()
    rows = stage[...]
    buf0[4, 4 * yh + x] = rows[:HALF, :LATENT]
    buf1[4, h] = jnp.concatenate(
        [rows[HALF:, :LATENT], rows[:HALF, LATENT:], rows[HALF:, LATENT:]], axis=1
    )
    targets = [
        (n, ahead, slot, flip)
        for n, (ahead, slot, flip) in enumerate(
            ((2, 2, 0), (2, 2, 1), (4, 0, 0), (4, 0, 1), (0, 4, 1))
        )
    ]
    for j in (1, 3, 2):
        remote(own_a, own_a, x_send.at[j - 1], x_recv.at[j - 1], along(j)).start()
    for n, ahead, slot, flip in targets:
        remote(own_b, buf1.at[slot, h], y_send.at[n], y_recv.at[n], across(ahead, flip)).start()

    def send_row(j):
        from_x = 4 * yh + jnp.bitwise_and(x - j, 3)
        if j:
            wait(own_a, x_recv.at[j - 1])
        for n, ahead, slot, flip in targets:
            remote(
                buf0.at[4, from_x], buf0.at[slot, from_x], row_send.at[5 * j + n],
                row_recv.at[slot], across(ahead, flip),
            ).start()

    def send_pair(n, slot, flip):
        from_y = 2 * x + yh + flip - 2 * yh * flip
        if n < 5:
            wait(own_b, y_recv.at[n])
        piece = buf1.at[slot, from_y]
        for j in (1, 3, 2):
            remote(piece, piece, pair_send.at[3 * n + j - 1], pair_recv.at[slot], along(j)).start()

    send_row(0)
    send_pair(5, 4, 0)
    send_row(1)
    send_row(3)
    pl.semaphore_wait(near_sem, 2)
    for ahead in (8, -8):
        pl.semaphore_signal(far_sem, inc=1, device_id=at(ahead), device_id_type=MESH)
    send_pair(0, 2, 0)
    send_pair(1, 2, 1)
    send_pair(2, 0, 0)
    send_pair(4, 4, 1)
    send_row(2)
    send_pair(3, 0, 1)

    for load in loads[:2]:
        load.wait()
    owner = owner_ref[...]
    row = lax.shift_right_logical(owner, 8)
    place_row = jnp.bitwise_and(owner, ROWS - 1)
    step_row = jnp.bitwise_and(row - c + (2 * N_CTX - 1), N_CTX - 1)
    step_all = jnp.broadcast_to(step_row, (ROWS, ROWS))
    sub = iota((ROWS, ROWS), 0)
    lane = iota((ROWS, ROWS), 1)
    step_col = jnp.sum(jnp.where(sub == lane, step_all, 0), axis=1, keepdims=True)
    same = (step_col == step_row) & (sub < lane)
    rank = jnp.sum(jnp.where(same, 1, 0), axis=0, keepdims=True)
    slot_row = step_row * SLOT + rank
    hit = sub == slot_row
    perm[...] = jnp.where(hit, 1.0, 0.0).astype(BF16)
    place_col = jnp.sum(jnp.where(hit, place_row, 0), axis=1, keepdims=True)
    place_slot = jnp.sum(jnp.where(sub == lane, place_col, 0), axis=0, keepdims=True)
    half_sub = iota((N_CTX // 2, 128), 0)
    half_lane = lax.shift_right_logical(iota((N_CTX // 2, 128), 1), 3)
    for part in range(2):
        spread = jnp.where(
            half_sub == half_lane, place_slot[:, part * 128 : (part + 1) * 128], 0
        )
        for j in range(N_CTX // 2):
            idx_out[part * N_CTX // 2 + j] = spread[j : j + 1]
    idx_in[N_CTX - 1] = idx_out[N_CTX - 1]

    lanes = iota((1, ROPE), 1)
    starts = jnp.zeros((1, ROPE), jnp.int32)
    ends = jnp.zeros((1, ROPE), jnp.int32)
    total = 0
    for d in range(DOCS):
        starts = jnp.where(lanes == d, total, starts)
        total = total + docs[d]
        ends = jnp.where(lanes == d, total, ends)
    step16 = iota((HALF_SPAN, ROPE), 0)
    within = jnp.bitwise_and(step16, 15)
    tile = jnp.bitwise_and(lax.shift_right_logical(step16, 4), 7)
    offset_a = jnp.bitwise_and(tile, 3) * 64 + lax.shift_right_logical(tile, 2) * 32 + within
    offset_b = tile * 32 + HALF + within
    block_pos = (c - 4 + lax.shift_right_logical(step16, 7)) * ROWS
    for half, offset in enumerate((offset_a, offset_b)):
        key_pos = block_pos + offset
        key_in = (key_pos >= starts) & (key_pos < ends)
        kbits[half] = jnp.where(
            key_in | (iota((HALF_SPAN, ROPE), 1) >= DOCS), 0.0, 1.0
        ).astype(BF16)
    query_pos = c * ROWS + iota((ROWS, ROPE), 0)
    query_in = (query_pos >= starts) & (query_pos < ends)
    query_bits = jnp.where(query_in, FAR, 0.0)
    zeros = jnp.zeros((ROWS, ROPE), F32)
    ones = jnp.ones((ROWS, ROPE), F32)
    qbits[0] = jnp.concatenate([zeros, query_bits], axis=1).astype(BF16)
    qbits[1] = jnp.concatenate([query_bits, zeros], axis=1).astype(BF16)
    qbits[2] = jnp.concatenate([ones, zeros], axis=1).astype(BF16)
    qbits[3] = jnp.concatenate([zeros, ones], axis=1).astype(BF16)

    def forward(buf, src, dst, n):
        remote(buf.at[src], buf.at[dst], fsend.at[n], frecv.at[n], sibling).start()

    def prepare(slot):
        latent = latents((slot,))
        cols = slice(0, 2 * NOPE)
        keys = jnp.dot(latent, ku[:, cols], preferred_element_type=F32).astype(BF16)
        values = jnp.dot(latent, vu[:, cols], preferred_element_type=F32).astype(BF16)
        rope = buf1[slot, :, :, LATENT:]
        for half in range(2):
            here = pl.ds(pl.multiple_of(half * HALF_SPAN + slot * 128, 128), 128)
            part = slice(half * 128, (half + 1) * 128)
            kv[0, 0, here] = keys[part]
            kv[0, 1, here] = values[part]
            if half == 0:
                rotary = jnp.concatenate([rope[n] for n in (0, 2, 4, 6, 1, 3, 5, 7)], axis=0)
            else:
                rotary = rope.reshape(128, 2 * ROPE)
            rotary = rotary[:, half * ROPE : (half + 1) * ROPE]
            bits = kbits[half, pl.ds(pl.multiple_of(slot * 128, 128), 128)]
            kr[0, here] = jnp.concatenate([rotary, bits], axis=1)
            kr[1, here] = jnp.concatenate([bits, rotary], axis=1)

    def latents(slots):
        return jnp.concatenate(
            [buf0[s].reshape(128, LATENT) for s in slots]
            + [buf1[s, :, :, :LATENT].reshape(128, LATENT) for s in slots],
            axis=0,
        )

    wait(buf0.at[2], row_recv.at[2])
    forward(buf0, 2, 2 * k + 1, 0)
    wait(buf1.at[2, pl.ds(0, 6)], pair_recv.at[2])
    forward(buf1, 2, 2 * k + 1, 1)
    for load in loads[2:]:
        load.wait()
    prepare(2)
    wait(buf0.at[4, pl.ds(0, 4)], row_recv.at[4])
    wait(buf0.at[0], row_recv.at[0])
    forward(buf0, 4 - 4 * k, 3 - 2 * k, 2)
    wait(buf1.at[4, pl.ds(0, 6)], pair_recv.at[4])
    prepare(4)
    wait(buf1.at[0, pl.ds(0, 6)], pair_recv.at[0])
    forward(buf1, 4 - 4 * k, 3 - 2 * k, 3)

    pl.semaphore_wait(far_sem, 2)
    for ahead in FAR_FIRST:
        remote(idx_out.at[ahead - 1], idx_in.at[ahead - 1], isend, irecv, at(ahead)).start()
    prepare(0)
    for n, slot in ((0, 3 - 2 * k), (2, 2 * k + 1)):
        wait(buf0.at[0], frecv.at[n])
        wait(buf1.at[0], frecv.at[n + 1])
        prepare(slot)

    query_row = iota((ROWS, 128), 0)
    key_lane = iota((ROWS, 128), 1)
    within = jnp.bitwise_and(key_lane, 15)
    tile = lax.shift_right_logical(key_lane, 4)
    lower = [
        jnp.bitwise_and(tile, 3) * 64 + lax.shift_right_logical(tile, 2) * 32 + within <= query_row,
        tile * 32 + HALF + within <= query_row,
    ]

    def attend(g, carry):
        cols = pl.ds(pl.multiple_of(g * 2 * NOPE, 2 * NOPE), 2 * NOPE)
        now = jnp.bitwise_and(g, 1)
        keys = kv[now, 0]
        values = kv[now, 1]
        q_two = qn[:, cols]
        r_two = qr[:, pl.ds(pl.multiple_of(g * 2 * ROPE, 2 * ROPE), 2 * ROPE)]
        outs = []
        for e in range(2):
            part = slice(e * NOPE, (e + 1) * NOPE)
            kx = jnp.concatenate([keys[:, part], kr[e]], axis=1)
            qx = jnp.concatenate([q_two[:, part], r_two * qbits[2 + e] + qbits[e]], axis=1)
            s = lax.dot_general(qx, kx, (((1,), (1,)), ((), ())), preferred_element_type=F32)
            parts = []
            for half in range(2):
                first = half * HALF_SPAN
                parts += [
                    jnp.where(lower[half], FAR, s[:, first : first + 128]),
                    s[:, first + 128 : first + 512],
                    jnp.where(lower[half], s[:, first + 512 : first + 640], FAR),
                ]
            s = jnp.concatenate(parts, axis=1)
            largest = jnp.max(s, axis=1, keepdims=True)
            p = jnp.exp2((s - largest) * TO_EXP2)
            weight = jnp.sum(p, axis=1, keepdims=True)
            o = jnp.dot(p.astype(BF16), values[:, part], preferred_element_type=F32)
            outs.append((o / weight).astype(BF16))
        both = jnp.concatenate(outs, axis=1)
        sorted_ = jnp.dot(perm[...], both, preferred_element_type=F32)
        sorted_ = sorted_.reshape(N_CTX, SLOT, 2 * NOPE)
        packed = jnp.concatenate([sorted_[:, :, :NOPE], sorted_[:, :, NOPE:]], axis=1).astype(BF16)
        outb[g] = packed
        inb[g, N_CTX - 1] = packed[N_CTX - 1]

        def send(ahead):
            remote(
                outb.at[g, ahead - 1], inb.at[g, ahead - 1], asend.at[g], arecv.at[g], at(ahead)
            ).start()

        @pl.when(g < GROUPS - 1)
        def far_first():
            for ahead in FAR_FIRST:
                send(ahead)

        @pl.when(g == GROUPS - 1)
        def in_order():
            for to in range(N_CTX):

                @pl.when(c != to)
                def send_to(to=to):
                    send(jnp.bitwise_and(to - c, N_CTX - 1))

        following = jnp.minimum(g + 1, GROUPS - 1) * 2 * NOPE
        cols = pl.ds(pl.multiple_of(following, 2 * NOPE), 2 * NOPE)
        latent = latents(range(BLOCKS))
        keys = jnp.dot(latent, ku[:, cols], preferred_element_type=F32)
        kv[1 - now, 0] = keys.astype(BF16)
        values = jnp.dot(latent, vu[:, cols], preferred_element_type=F32)
        kv[1 - now, 1] = values.astype(BF16)
        return carry

    lax.fori_loop(0, GROUPS, attend, 0)

    rest = pl.ds(0, N_CTX - 1)
    wait(idx_in.at[rest], irecv)
    goals = []
    for part in range(2):
        goal = idx_in[part * N_CTX // 2]
        for j in range(1, N_CTX // 2):
            goal = goal + idx_in[part * N_CTX // 2 + j]
        goals.append(goal)
    place[...] = jnp.where(jnp.concatenate(goals, axis=1) == sub, 1.0, 0.0).astype(BF16)

    def settle(g, carry):
        cols = pl.ds(pl.multiple_of(g * 2 * NOPE, 2 * NOPE), 2 * NOPE)
        wait(inb.at[g, rest], arecv.at[g])
        got = inb[g].astype(F32)
        got = jnp.concatenate([got[:, :SLOT], got[:, SLOT:]], axis=2).reshape(ROWS, 2 * NOPE)
        out_ref[:, cols] = jnp.dot(
            place[...], got.astype(BF16), preferred_element_type=F32
        ).astype(BF16)
        return carry

    lax.fori_loop(0, GROUPS, settle, 0)

    for n in range(3):
        wait(own_a, x_send.at[n])
    for n in range(5):
        wait(own_b, y_send.at[n])
    for n in range(20):
        wait(own_a, row_send.at[n])
    for n in range(18):
        wait(own_b, pair_send.at[n])
    for n in range(4):
        wait((buf0, buf1)[n % 2].at[0], fsend.at[n])
    wait(idx_out.at[rest], isend)

    def all_sent(g, carry):
        wait(outb.at[g, rest], asend.at[g])
        return carry

    lax.fori_loop(0, GROUPS, all_sent, 0)


def per_device(query_nope, query_rope, latent, key_up, value_up, doc_lengths, owner):
    hbm = pl.BlockSpec(memory_space=pltpu.HBM)
    dma = pltpu.SemaphoreType.DMA
    regular = pltpu.SemaphoreType.REGULAR
    args = (query_nope, query_rope, latent, key_up, value_up, doc_lengths, owner.reshape(1, ROWS))
    return pl.pallas_call(
        kernel,
        out_shape=pltpu.VMEM(query_nope.shape, BF16),
        in_specs=[hbm] * len(args),
        out_specs=pl.BlockSpec(memory_space=pltpu.VMEM),
        scratch_shapes=[
            pltpu.SMEM((DOCS,), jnp.int32),
            pltpu.VMEM((1, ROWS), jnp.int32),
            pltpu.VMEM(query_nope.shape, BF16),
            pltpu.VMEM(query_rope.shape, BF16),
            pltpu.VMEM(key_up.shape, BF16),
            pltpu.VMEM(value_up.shape, BF16),
            pltpu.VMEM((2 * HALF, LATENT + ROPE), BF16),
            pltpu.VMEM((BLOCKS, N_HEAD, HALF, LATENT), BF16),
            pltpu.VMEM((BLOCKS, N_HEAD, HALF, LATENT + 2 * ROPE), BF16),
            pltpu.VMEM((2, 2, SPAN, 2 * NOPE), BF16),
            pltpu.VMEM((2, SPAN, 2 * ROPE), BF16),
            pltpu.VMEM((2, HALF_SPAN, ROPE), BF16),
            pltpu.VMEM((4, ROWS, 2 * ROPE), BF16),
            pltpu.VMEM((ROWS, ROWS), BF16),
            pltpu.VMEM((ROWS, ROWS), BF16),
            pltpu.VMEM((GROUPS, N_CTX, 2 * SLOT, NOPE), BF16),
            pltpu.VMEM((GROUPS, N_CTX, 2 * SLOT, NOPE), BF16),
            pltpu.VMEM((N_CTX, 1, 128), jnp.int32),
            pltpu.VMEM((N_CTX, 1, 128), jnp.int32),
            dma((6,)),
            dma,
            dma((3,)),
            dma((5,)),
            dma((20,)),
            dma((18,)),
            dma((3,)),
            dma((5,)),
            dma((5,)),
            dma((5,)),
            dma((4,)),
            dma((4,)),
            dma,
            dma,
            dma((GROUPS,)),
            dma((GROUPS,)),
            regular,
            regular,
        ],
        compiler_params=pltpu.CompilerParams(
            collective_id=0, has_side_effects=True, vmem_limit_bytes=48 << 20
        ),
        name="attend_and_place",
    )(*[pltpu.with_memory_space_constraint(a, pltpu.HBM) for a in args])


def solution(mesh):
    in_specs = (
        P("ctx", "head"),
        P("ctx", "head"),
        P(("ctx", "head"), None),
        P(None, "head"),
        P(None, "head"),
        P(),
        P("ctx"),
    )
    return jax.shard_map(
        per_device, mesh=mesh, in_specs=in_specs, out_specs=P("ctx", "head"), check_vma=False
    )
```

```python
import functools

import jax
import jax.numpy as jnp
from jax import lax
from jax.experimental import pallas as pl
from jax.experimental.pallas import tpu as pltpu
from jax.sharding import PartitionSpec as P

LATENT = 512
ROPE = 64
NOPE = 128
ROWS = 256
N_CTX = 32
N_HEAD = 8
HALF = 16
BLOCKS = 5
SPAN = BLOCKS * ROWS
HALF_SPAN = SPAN // 2
WINDOW = 1024
GROUPS = 8
SLOT = 8
DOCS = 8
FAR = -1e30
TO_EXP2 = 1.4426950408889634 / float(NOPE + ROPE) ** 0.5
FAR_FIRST = sorted(range(1, N_CTX), key=lambda ahead: abs(ahead - N_CTX // 2))
RELAYED = {5: 1, 0: 3}
MESH = pl.DeviceIdType.MESH
F32 = jnp.float32
BF16 = jnp.bfloat16


def iota(shape, dim):
    return lax.broadcasted_iota(jnp.int32, shape, dim)


def kernel(
    qn_hbm, qr_hbm, lat_hbm, ku_hbm, vu_hbm, docs_hbm, owner_hbm, out_ref,
    docs, owner_ref, qn, qr, ku, vu, stage, buf0, buf1, kv, kr, kbits, qbits, perm, place, outb, inb, idx_out, idx_in,
    load_sem, lat_sem, x_send, y_send, row_send, pair_send, x_recv, y_recv, row_recv, pair_recv, relay_recv,
    fsend, frecv, isend, irecv, asend, arecv, near_sem, far_sem,
):
    c = lax.axis_index("ctx")
    h = lax.axis_index("head")
    k = jnp.bitwise_and(c, 1)
    x = h // 2
    yh = jnp.bitwise_and(h, 1)
    sibling = (c + 1 - 2 * k, h)

    def at(ahead):
        return (jnp.bitwise_and(c + ahead + N_CTX, N_CTX - 1), h)

    def across(ahead, flip):
        return (jnp.bitwise_and(c + ahead + N_CTX, N_CTX - 1), 2 * x + yh + flip - 2 * yh * flip)

    def along(j):
        return (c, 2 * jnp.bitwise_and(x + j, 3) + yh)

    def remote(src, dst, send, recv, to):
        return pltpu.make_async_remote_copy(
            src, dst, send, recv, device_id=to, device_id_type=MESH
        )

    def wait(ref, sem):
        pltpu.make_async_copy(ref, ref, sem).wait()

    own_a = buf0.at[4, 4 * yh + x]
    own_b = buf1.at[4, h]
    lat_in = pltpu.make_async_copy(lat_hbm, stage, lat_sem)
    loads = [
        pltpu.make_async_copy(src, dst, load_sem.at[i])
        for i, (src, dst) in enumerate(
            (
                (owner_hbm, owner_ref), (docs_hbm, docs), (ku_hbm, ku), (vu_hbm, vu),
                (qn_hbm, qn), (qr_hbm, qr),
            )
        )
    ]
    for load in [lat_in] + loads:
        load.start()

    barrier = pltpu.get_barrier_semaphore()
    met = 0
    for plane in (0, -4, 4):
        for j in range(4):
            if plane or j:
                to = jnp.bitwise_and(c + plane + N_CTX, N_CTX - 4) + jnp.bitwise_and(c + j, 3)
                pl.semaphore_signal(barrier, inc=1, device_id=(to, h), device_id_type=MESH)
                met += 1
    for j in (1, 2, 3):
        pl.semaphore_signal(barrier, inc=1, device_id=along(j), device_id_type=MESH)
        met += 1
    for ahead in (0, 2, -2, 4, -4):
        pl.semaphore_signal(barrier, inc=1, device_id=across(ahead, 1), device_id_type=MESH)
        met += 1
    pl.semaphore_wait(barrier, met)
    for ahead in (4, -4):
        pl.semaphore_signal(near_sem, inc=1, device_id=at(ahead), device_id_type=MESH)

    lat_in.wait()
    rows = stage[...]
    buf0[4, 4 * yh + x] = rows[:HALF, :LATENT]
    buf1[4, h] = jnp.concatenate(
        [rows[HALF:, :LATENT], rows[:HALF, LATENT:], rows[HALF:, LATENT:]], axis=1
    )
    targets = [
        (n, ahead, slot, flip)
        for n, (ahead, slot, flip) in enumerate(
            ((2, 2, 0), (2, 2, 1), (4, 0, 0), (4, 0, 1), (0, 4, 1))
        )
    ]
    for j in (1, 3, 2):
        remote(own_a, own_a, x_send.at[j - 1], x_recv.at[j - 1], along(j)).start()
    for n, ahead, slot, flip in targets:
        remote(own_b, buf1.at[slot, h], y_send.at[n], y_recv.at[n], across(ahead, flip)).start()

    def send_row(j):
        from_x = 4 * yh + jnp.bitwise_and(x - j, 3)
        if j:
            wait(own_a, x_recv.at[j - 1])
        for n, ahead, slot, flip in targets:
            remote(
                buf0.at[4, from_x], buf0.at[slot, from_x], row_send.at[5 * j + n],
                row_recv.at[slot], across(ahead, flip),
            ).start()

    def send_pair(n, slot, flip):
        from_y = 2 * x + yh + flip - 2 * yh * flip
        if n < 5:
            wait(own_b, y_recv.at[n])
        piece = buf1.at[slot, from_y]
        way = RELAYED.get(n, 0)
        for j in (1, 3, 2):
            if way and j == 2:
                continue
            landed = relay_recv.at[way // 2] if j == way else pair_recv.at[slot]
            remote(piece, piece, pair_send.at[3 * n + j - 1], landed, along(j)).start()

    def relay(n, slot):
        way = RELAYED[n]
        wait(own_b, relay_recv.at[way // 2])
        piece = buf1.at[slot, 2 * jnp.bitwise_and(x - way, 3) + yh]
        remote(piece, piece, pair_send.at[3 * n + 1], pair_recv.at[slot], along(way)).start()

    send_row(0)
    send_pair(5, 4, 0)
    send_row(1)
    send_row(3)
    pl.semaphore_wait(near_sem, 2)
    for ahead in (8, -8):
        pl.semaphore_signal(far_sem, inc=1, device_id=at(ahead), device_id_type=MESH)
    send_pair(0, 2, 0)
    relay(5, 4)
    send_pair(1, 2, 1)
    send_pair(2, 0, 0)
    send_pair(4, 4, 1)
    relay(0, 2)
    send_row(2)
    send_pair(3, 0, 1)

    for load in loads[:2]:
        load.wait()
    owner = owner_ref[...]
    row = lax.shift_right_logical(owner, 8)
    place_row = jnp.bitwise_and(owner, ROWS - 1)
    step_row = jnp.bitwise_and(row - c + (2 * N_CTX - 1), N_CTX - 1)
    step_all = jnp.broadcast_to(step_row, (ROWS, ROWS))
    sub = iota((ROWS, ROWS), 0)
    lane = iota((ROWS, ROWS), 1)
    step_col = jnp.sum(jnp.where(sub == lane, step_all, 0), axis=1, keepdims=True)
    same = (step_col == step_row) & (sub < lane)
    rank = jnp.sum(jnp.where(same, 1, 0), axis=0, keepdims=True)
    slot_row = step_row * SLOT + rank
    hit = sub == slot_row
    perm[...] = jnp.where(hit, 1.0, 0.0).astype(BF16)
    place_col = jnp.sum(jnp.where(hit, place_row, 0), axis=1, keepdims=True)
    place_slot = jnp.sum(jnp.where(sub == lane, place_col, 0), axis=0, keepdims=True)
    half_sub = iota((N_CTX // 2, 128), 0)
    half_lane = lax.shift_right_logical(iota((N_CTX // 2, 128), 1), 3)
    for part in range(2):
        spread = jnp.where(
            half_sub == half_lane, place_slot[:, part * 128 : (part + 1) * 128], 0
        )
        for j in range(N_CTX // 2):
            idx_out[part * N_CTX // 2 + j] = spread[j : j + 1]
    idx_in[N_CTX - 1] = idx_out[N_CTX - 1]

    lanes = iota((1, ROPE), 1)
    starts = jnp.zeros((1, ROPE), jnp.int32)
    ends = jnp.zeros((1, ROPE), jnp.int32)
    total = 0
    for d in range(DOCS):
        starts = jnp.where(lanes == d, total, starts)
        total = total + docs[d]
        ends = jnp.where(lanes == d, total, ends)
    step16 = iota((HALF_SPAN, ROPE), 0)
    within = jnp.bitwise_and(step16, 15)
    tile = jnp.bitwise_and(lax.shift_right_logical(step16, 4), 7)
    offset_a = jnp.bitwise_and(tile, 3) * 64 + lax.shift_right_logical(tile, 2) * 32 + within
    offset_b = tile * 32 + HALF + within
    block_pos = (c - 4 + lax.shift_right_logical(step16, 7)) * ROWS
    for half, offset in enumerate((offset_a, offset_b)):
        key_pos = block_pos + offset
        key_in = (key_pos >= starts) & (key_pos < ends)
        kbits[half] = jnp.where(
            key_in | (iota((HALF_SPAN, ROPE), 1) >= DOCS), 0.0, 1.0
        ).astype(BF16)
    query_pos = c * ROWS + iota((ROWS, ROPE), 0)
    query_in = (query_pos >= starts) & (query_pos < ends)
    query_bits = jnp.where(query_in, FAR, 0.0)
    zeros = jnp.zeros((ROWS, ROPE), F32)
    ones = jnp.ones((ROWS, ROPE), F32)
    qbits[0] = jnp.concatenate([zeros, query_bits], axis=1).astype(BF16)
    qbits[1] = jnp.concatenate([query_bits, zeros], axis=1).astype(BF16)
    qbits[2] = jnp.concatenate([ones, zeros], axis=1).astype(BF16)
    qbits[3] = jnp.concatenate([zeros, ones], axis=1).astype(BF16)

    def forward(buf, src, dst, n):
        remote(buf.at[src], buf.at[dst], fsend.at[n], frecv.at[n], sibling).start()

    def prepare(slot):
        latent = latents((slot,))
        cols = slice(0, 2 * NOPE)
        keys = jnp.dot(latent, ku[:, cols], preferred_element_type=F32).astype(BF16)
        values = jnp.dot(latent, vu[:, cols], preferred_element_type=F32).astype(BF16)
        rope = buf1[slot, :, :, LATENT:]
        for half in range(2):
            here = pl.ds(pl.multiple_of(half * HALF_SPAN + slot * 128, 128), 128)
            part = slice(half * 128, (half + 1) * 128)
            kv[0, 0, here] = keys[part]
            kv[0, 1, here] = values[part]
            if half == 0:
                rotary = jnp.concatenate([rope[n] for n in (0, 2, 4, 6, 1, 3, 5, 7)], axis=0)
            else:
                rotary = rope.reshape(128, 2 * ROPE)
            rotary = rotary[:, half * ROPE : (half + 1) * ROPE]
            bits = kbits[half, pl.ds(pl.multiple_of(slot * 128, 128), 128)]
            kr[0, here] = jnp.concatenate([rotary, bits], axis=1)
            kr[1, here] = jnp.concatenate([bits, rotary], axis=1)

    def latents(slots):
        return jnp.concatenate(
            [buf0[s].reshape(128, LATENT) for s in slots]
            + [buf1[s, :, :, :LATENT].reshape(128, LATENT) for s in slots],
            axis=0,
        )

    wait(buf0.at[2], row_recv.at[2])
    forward(buf0, 2, 2 * k + 1, 0)
    wait(buf1.at[2, pl.ds(0, 5)], pair_recv.at[2])
    forward(buf1, 2, 2 * k + 1, 1)
    for load in loads[2:]:
        load.wait()
    prepare(2)
    wait(buf0.at[4, pl.ds(0, 4)], row_recv.at[4])
    wait(buf0.at[0], row_recv.at[0])
    forward(buf0, 4 - 4 * k, 3 - 2 * k, 2)
    wait(buf1.at[4, pl.ds(0, 5)], pair_recv.at[4])
    prepare(4)
    wait(buf1.at[0, pl.ds(0, 6)], pair_recv.at[0])
    forward(buf1, 4 - 4 * k, 3 - 2 * k, 3)

    pl.semaphore_wait(far_sem, 2)
    for ahead in FAR_FIRST:
        remote(idx_out.at[ahead - 1], idx_in.at[ahead - 1], isend, irecv, at(ahead)).start()
    prepare(0)
    for n, slot in ((0, 3 - 2 * k), (2, 2 * k + 1)):
        wait(buf0.at[0], frecv.at[n])
        wait(buf1.at[0], frecv.at[n + 1])
        prepare(slot)

    query_row = iota((ROWS, 128), 0)
    key_lane = iota((ROWS, 128), 1)
    within = jnp.bitwise_and(key_lane, 15)
    tile = lax.shift_right_logical(key_lane, 4)
    lower = [
        jnp.bitwise_and(tile, 3) * 64 + lax.shift_right_logical(tile, 2) * 32 + within <= query_row,
        tile * 32 + HALF + within <= query_row,
    ]

    def attend(g, carry):
        cols = pl.ds(pl.multiple_of(g * 2 * NOPE, 2 * NOPE), 2 * NOPE)
        now = jnp.bitwise_and(g, 1)
        keys = kv[now, 0]
        values = kv[now, 1]
        q_two = qn[:, cols]
        r_two = qr[:, pl.ds(pl.multiple_of(g * 2 * ROPE, 2 * ROPE), 2 * ROPE)]
        outs = []
        for e in range(2):
            part = slice(e * NOPE, (e + 1) * NOPE)
            kx = jnp.concatenate([keys[:, part], kr[e]], axis=1)
            qx = jnp.concatenate([q_two[:, part], r_two * qbits[2 + e] + qbits[e]], axis=1)
            s = lax.dot_general(qx, kx, (((1,), (1,)), ((), ())), preferred_element_type=F32)
            parts = []
            for half in range(2):
                first = half * HALF_SPAN
                parts += [
                    jnp.where(lower[half], FAR, s[:, first : first + 128]),
                    s[:, first + 128 : first + 512],
                    jnp.where(lower[half], s[:, first + 512 : first + 640], FAR),
                ]
            s = jnp.concatenate(parts, axis=1)
            largest = jnp.max(s, axis=1, keepdims=True)
            p = jnp.exp2((s - largest) * TO_EXP2)
            weight = jnp.sum(p, axis=1, keepdims=True)
            o = jnp.dot(p.astype(BF16), values[:, part], preferred_element_type=F32)
            outs.append((o / weight).astype(BF16))
        both = jnp.concatenate(outs, axis=1)
        sorted_ = jnp.dot(perm[...], both, preferred_element_type=F32)
        sorted_ = sorted_.reshape(N_CTX, SLOT, 2 * NOPE)
        packed = jnp.concatenate([sorted_[:, :, :NOPE], sorted_[:, :, NOPE:]], axis=1).astype(BF16)
        outb[g] = packed
        inb[g, N_CTX - 1] = packed[N_CTX - 1]

        def send(ahead):
            remote(
                outb.at[g, ahead - 1], inb.at[g, ahead - 1], asend.at[g], arecv.at[g], at(ahead)
            ).start()

        @pl.when(g < GROUPS - 1)
        def far_first():
            for ahead in FAR_FIRST:
                send(ahead)

        @pl.when(g == GROUPS - 1)
        def in_order():
            for to in range(N_CTX):

                @pl.when(c != to)
                def send_to(to=to):
                    send(jnp.bitwise_and(to - c, N_CTX - 1))

        following = jnp.minimum(g + 1, GROUPS - 1) * 2 * NOPE
        cols = pl.ds(pl.multiple_of(following, 2 * NOPE), 2 * NOPE)
        latent = latents(range(BLOCKS))
        keys = jnp.dot(latent, ku[:, cols], preferred_element_type=F32)
        kv[1 - now, 0] = keys.astype(BF16)
        values = jnp.dot(latent, vu[:, cols], preferred_element_type=F32)
        kv[1 - now, 1] = values.astype(BF16)
        return carry

    lax.fori_loop(0, GROUPS, attend, 0)

    rest = pl.ds(0, N_CTX - 1)
    wait(idx_in.at[rest], irecv)
    goals = []
    for part in range(2):
        goal = idx_in[part * N_CTX // 2]
        for j in range(1, N_CTX // 2):
            goal = goal + idx_in[part * N_CTX // 2 + j]
        goals.append(goal)
    place[...] = jnp.where(jnp.concatenate(goals, axis=1) == sub, 1.0, 0.0).astype(BF16)

    def settle(g, carry):
        cols = pl.ds(pl.multiple_of(g * 2 * NOPE, 2 * NOPE), 2 * NOPE)
        wait(inb.at[g, rest], arecv.at[g])
        got = inb[g].astype(F32)
        got = jnp.concatenate([got[:, :SLOT], got[:, SLOT:]], axis=2).reshape(ROWS, 2 * NOPE)
        out_ref[:, cols] = jnp.dot(
            place[...], got.astype(BF16), preferred_element_type=F32
        ).astype(BF16)
        return carry

    lax.fori_loop(0, GROUPS, settle, 0)

    for n in range(3):
        wait(own_a, x_send.at[n])
    for n in range(5):
        wait(own_b, y_send.at[n])
    for n in range(20):
        wait(own_a, row_send.at[n])
    for n in range(18):
        wait(own_b, pair_send.at[n])
    for n in range(4):
        wait((buf0, buf1)[n % 2].at[0], fsend.at[n])
    wait(idx_out.at[rest], isend)

    def all_sent(g, carry):
        wait(outb.at[g, rest], asend.at[g])
        return carry

    lax.fori_loop(0, GROUPS, all_sent, 0)


def per_device(query_nope, query_rope, latent, key_up, value_up, doc_lengths, owner):
    hbm = pl.BlockSpec(memory_space=pltpu.HBM)
    dma = pltpu.SemaphoreType.DMA
    regular = pltpu.SemaphoreType.REGULAR
    args = (query_nope, query_rope, latent, key_up, value_up, doc_lengths, owner.reshape(1, ROWS))
    return pl.pallas_call(
        kernel,
        out_shape=pltpu.VMEM(query_nope.shape, BF16),
        in_specs=[hbm] * len(args),
        out_specs=pl.BlockSpec(memory_space=pltpu.VMEM),
        scratch_shapes=[
            pltpu.SMEM((DOCS,), jnp.int32),
            pltpu.VMEM((1, ROWS), jnp.int32),
            pltpu.VMEM(query_nope.shape, BF16),
            pltpu.VMEM(query_rope.shape, BF16),
            pltpu.VMEM(key_up.shape, BF16),
            pltpu.VMEM(value_up.shape, BF16),
            pltpu.VMEM((2 * HALF, LATENT + ROPE), BF16),
            pltpu.VMEM((BLOCKS, N_HEAD, HALF, LATENT), BF16),
            pltpu.VMEM((BLOCKS, N_HEAD, HALF, LATENT + 2 * ROPE), BF16),
            pltpu.VMEM((2, 2, SPAN, 2 * NOPE), BF16),
            pltpu.VMEM((2, SPAN, 2 * ROPE), BF16),
            pltpu.VMEM((2, HALF_SPAN, ROPE), BF16),
            pltpu.VMEM((4, ROWS, 2 * ROPE), BF16),
            pltpu.VMEM((ROWS, ROWS), BF16),
            pltpu.VMEM((ROWS, ROWS), BF16),
            pltpu.VMEM((GROUPS, N_CTX, 2 * SLOT, NOPE), BF16),
            pltpu.VMEM((GROUPS, N_CTX, 2 * SLOT, NOPE), BF16),
            pltpu.VMEM((N_CTX, 1, 128), jnp.int32),
            pltpu.VMEM((N_CTX, 1, 128), jnp.int32),
            dma((6,)),
            dma,
            dma((3,)),
            dma((5,)),
            dma((20,)),
            dma((18,)),
            dma((3,)),
            dma((5,)),
            dma((5,)),
            dma((5,)),
            dma((2,)),
            dma((4,)),
            dma((4,)),
            dma,
            dma,
            dma((GROUPS,)),
            dma((GROUPS,)),
            regular,
            regular,
        ],
        compiler_params=pltpu.CompilerParams(
            collective_id=0, has_side_effects=True, vmem_limit_bytes=48 << 20
        ),
        name="attend_and_place",
    )(*[pltpu.with_memory_space_constraint(a, pltpu.HBM) for a in args])


def solution(mesh):
    in_specs = (
        P("ctx", "head"),
        P("ctx", "head"),
        P(("ctx", "head"), None),
        P(None, "head"),
        P(None, "head"),
        P(),
        P("ctx"),
    )
    return jax.shard_map(
        per_device, mesh=mesh, in_specs=in_specs, out_specs=P("ctx", "head"), check_vma=False
    )
```
